256 devices in a mesh: row: 32 (over y, z), col: 8 (over x, core).
Axes of the slice: x: 4, y: 4, z: 8, core: 2. Of those that a mesh axis runs over, the one named last changes fastest.
Arguments:
- diag_tile: float32 [2048, 2048], P('row', 'col'), as said below
- rows_left: bfloat16 [32, 2048, 256], P('row', None, 'col'), may hold values from -6 to 6
- rows_right: bfloat16 [32, 2048, 256], P('row', None, 'col'), may hold values from -0.375 to 0.375
- rows_rank: int32 [32], P('row'), may hold values from 32 to 256, as said below
- cols_right: bfloat16 [8, 2048, 256], P('col', None, 'row'), may hold values from -0.375 to 0.375
- cols_rank: int32 [8], P('col'), may hold values from 32 to 256, as said below
Outputs:
- appended_left: bfloat16 [32, 8, 2048, 256], P('row', 'col')
- solved_rows: bfloat16 [32, 2048, 256], P('row', None, 'col')
The draws below stay inside these ranges and needn't reach their ends.
Inputs may be any that keep to these rules, and one draw needn't show every extreme that they name: `rows_rank`: every rank is a multiple of 32; some row-panel tile has rank 256. `cols_rank`: every rank is a multiple of 32; some column-panel tile has rank 256. diag_tile is symmetric positive definite.
All inputs are finite; a program needn't handle non-finite values.
Results may differ from the reference program's by a relative error of at most 0.0063.
Values may be sent and summed in bfloat16 or wider, within the bound.
A program may use at most 256 MiB of HBM per device.

```python
import jax
import jax.numpy as jnp
from jax import lax

NB = 2048
RMAX = 256
PANEL_ROWS = 32
PANEL_COLS = 8


rank_unit = 32


def draw_diag_tile(key, part):
    key = jax.random.fold_in(key, 11)
    key_points, key_noise = jax.random.split(key)
    points = jax.random.uniform(key_points, (NB, 3), jnp.float32)
    delta_x = points[:, None, 0] - points[None, :, 0]
    delta_y = points[:, None, 1] - points[None, :, 1]
    delta_z = points[:, None, 2] - points[None, :, 2]
    distance = jnp.sqrt(delta_x * delta_x + delta_y * delta_y + delta_z * delta_z)
    scaled = jnp.sqrt(3.0) * distance * float(NB) ** (1.0 / 3.0) / 1.5
    kernel = (1.0 + scaled) * jnp.exp(-scaled)
    identity = jnp.eye(NB, dtype=jnp.float32)
    raw = jax.random.uniform(key_noise, (NB, NB), jnp.float32, -1.0, 1.0) * (0.5 / NB)
    noise = 0.5 * (raw + raw.T) * (1.0 - identity) + 0.5 * identity
    return kernel + noise + identity


def rank_list(key, count):
    key_ranks, key_place = jax.random.split(key)
    ranks = rank_unit * jax.random.randint(key_ranks, (count,), 1, RMAX // rank_unit + 1)
    place = jax.random.randint(key_place, (), 0, count)
    return ranks.at[place].set(RMAX).astype(jnp.int32)


def draw_rows_rank(key, part):
    key = jax.random.fold_in(key, 21)
    return rank_list(key, PANEL_ROWS)


def draw_cols_rank(key, part):
    key = jax.random.fold_in(key, 31)
    return rank_list(key, PANEL_COLS)


def level_of(key, shape, shards, smallest, high):
    factor_of = 1.0
    for axis_at, shards_of in shards:
        steps = jax.random.uniform(jax.random.fold_in(jax.random.fold_in(key, 6), axis_at), (shards_of,), jnp.float32, smallest / len(shards), high / len(shards))
        factor_of = factor_of * jnp.repeat(jnp.exp(steps), shape[axis_at] // shards_of).reshape((-1,) + (1,) * (len(shape) - 1 - axis_at))
    return factor_of


def bell_draw(rng, extent, width, limit, shards=(), kind=jnp.bfloat16):
    loudness = level_of(rng, extent, shards, -0.22, 0.18) if shards else 1.0
    result = jax.random.normal(rng, extent, jnp.float32) * width * loudness
    return jnp.minimum(jnp.maximum(result, -limit), limit).astype(kind)


def setup_inputs(seed: int = 0) -> dict:
    arg_keys = jax.random.split(jax.random.key(seed), 7)
    return {
        "diag_tile": draw_diag_tile(jax.random.fold_in(arg_keys[6], 71), 0),
        "rows_left": bell_draw(arg_keys[1], (PANEL_ROWS, NB, RMAX), 1.0, 6.0, ((0, 32), (2, 8))),
        "rows_right": bell_draw(arg_keys[2], (PANEL_ROWS, NB, RMAX), (NB // 8) ** -0.5, 0.375, ((0, 32), (2, 8))),
        "rows_rank": draw_rows_rank(jax.random.fold_in(arg_keys[6], 71), 0),
        "cols_right": bell_draw(arg_keys[4], (PANEL_COLS, NB, RMAX), (NB // 8) ** -0.5, 0.375, ((0, 8), (2, 32))),
        "cols_rank": draw_cols_rank(jax.random.fold_in(arg_keys[6], 71), 0),
    }


def mask_rank(factor, rank_value):
    columns = jnp.arange(factor.shape[-1], dtype=jnp.int32)
    return jnp.where(columns[None, :] < rank_value, factor, jnp.zeros_like(factor))

def reference(diag_tile, rows_left, rows_right, rows_rank, cols_right, cols_rank):
    factor_low = jnp.linalg.cholesky(diag_tile)

    def solve_one(pair):
        factor, rank_value = pair
        masked = mask_rank(factor, rank_value).astype(jnp.float32)
        solved = jax.scipy.linalg.solve_triangular(factor_low, masked, lower=True)
        return solved.astype(jnp.bfloat16)
    solved_rows = lax.map(solve_one, (rows_right, rows_rank))
    solved_cols = lax.map(solve_one, (cols_right, cols_rank))
    solved_cols_wide = solved_cols.astype(jnp.float32)

    def row_update(pair):
        left, right = (pair[0], pair[1])
        left_masked = mask_rank(left, pair[2]).astype(jnp.float32)
        core = jnp.einsum('nr,cns->crs', right.astype(jnp.float32), solved_cols_wide).astype(jnp.bfloat16)
        update = jnp.einsum('nr,crs->cns', left_masked, core.astype(jnp.float32))
        return (-update).astype(jnp.bfloat16)
    appended_left = lax.map(row_update, (rows_left, solved_rows, rows_rank))
    return (appended_left, solved_rows)
```

```python
import functools

import jax
import jax.numpy as jnp
from jax import lax
from jax.experimental import pallas as pl
from jax.experimental.pallas import tpu as pltpu
from jax.sharding import PartitionSpec as P

f32 = jnp.float32
bf16 = jnp.bfloat16
ORDER = 2048
WIDE = 256
HALF = 128
STEPS = ORDER // WIDE


def split(x):
    high = x.astype(bf16)
    return high, (x - high.astype(f32)).astype(bf16)


def dot_nt(a, b):
    return lax.dot_general(a, b, (((1,), (1,)), ((), ())), preferred_element_type=f32)


def dot_nn(a, b):
    return lax.dot_general(a, b, (((1,), (0,)), ((), ())), preferred_element_type=f32)


def dot_tn(a, b):
    return lax.dot_general(a, b, (((0,), (0,)), ((), ())), preferred_element_type=f32)


def dot3(dot, a, b):
    return dot(a[0], b[0]) + (dot(a[0], b[1]) + dot(a[1], b[0]))


def invert_factor(s_ref, w_ref):
    lane = lax.broadcasted_iota(jnp.int32, (8, HALF), 1)
    sub = lax.broadcasted_iota(jnp.int32, (8, HALF), 0)
    for group in range(HALF // 8):
        first = 8 * group
        rows = s_ref[first : first + 8, :]
        in_group = (lane >= first) & (lane < first + 8)
        columns = [jnp.broadcast_to(rows[:, first + c : first + c + 1], (8, HALF)) for c in range(8)]
        g = {}
        for c in range(8):
            for r in range(c + 1):
                g[r, c] = jnp.broadcast_to(columns[c][r : r + 1, :], (8, HALF))
        inverse = []
        factor = {}
        for k in range(8):
            inverse.append(1.0 / g[k, k])
            for c in range(k + 1, 8):
                factor[k, c] = g[k, c] * inverse[k]
            for r in range(k + 1, 8):
                for c in range(r, 8):
                    g[r, c] = g[r, c] - factor[k, r] * g[k, c]
        start = jnp.where(in_group, (lane - first == sub).astype(f32), rows)
        pivot_rows = []
        for k in range(8):
            row = jnp.broadcast_to(start[k : k + 1, :], (8, HALF))
            for j in range(k):
                row = row - factor[j, k] * pivot_rows[j]
            pivot_rows.append(row)
        done = jnp.zeros((8, HALF), f32)
        for k in range(8):
            done = jnp.where(sub == k, pivot_rows[k] * lax.rsqrt(g[k, k]), done)
        w_ref[first : first + 8, :] = jnp.where(lane - first <= sub, done, 0.0)
        for below in range(group + 1, HALF // 8):
            block = s_ref[8 * below : 8 * below + 8, :]
            m = []
            for c in range(8):
                value = jnp.broadcast_to(block[:, first + c : first + c + 1], (8, HALF))
                for j in range(c):
                    value = value - m[j] * g[j, c]
                m.append(value * inverse[c])
            block = jnp.where(in_group, 0.0, block)
            for c in range(8):
                block = block - m[c] * pivot_rows[c]
            s_ref[8 * below : 8 * below + 8, :] = block


def factor_kernel(
    a_hbm, lh_hbm, ll_hbm, wh_ref, wl_ref, a_ref, lh_ref, ll_ref, d_ref, s_ref, w1_ref, w2_ref, in_sem, out_sem
):
    def arrive(k):
        at = pl.ds(k * WIDE, ORDER - k * WIDE)
        return pltpu.make_async_copy(
            a_hbm.at[at, pl.ds(k * WIDE, WIDE)], a_ref.at[at, pl.ds(k * WIDE, WIDE)], in_sem.at[k]
        )

    def leave(k, which):
        at = pl.ds((k + 1) * WIDE, ORDER - (k + 1) * WIDE)
        source, target = ((lh_ref, lh_hbm), (ll_ref, ll_hbm))[which]
        return pltpu.make_async_copy(
            source.at[at, pl.ds(k * WIDE, WIDE)], target.at[at, pl.ds(k * WIDE, WIDE)], out_sem.at[which, k]
        )

    for k in range(STEPS):
        arrive(k).start()

    def earlier(k, rows):
        here = pl.ds(k * WIDE, WIDE)
        done = pl.ds(0, k * WIDE)
        return dot3(
            dot_nt, (lh_ref[rows, done], ll_ref[rows, done]), (lh_ref[here, done], ll_ref[here, done])
        )

    def half(h, carry):
        k = h // 2
        odd = h % 2

        for static in range(STEPS):

            @pl.when((k == static) & (odd == 0))
            def _():
                here = pl.ds(static * WIDE, WIDE)
                arrive(static).wait()
                block = a_ref[here, here]
                if static:
                    block = block - earlier(static, here)
                d_ref[...] = block
                s_ref[...] = block[:HALF, :HALF]

        @pl.when(odd == 1)
        def _():
            low = dot3(dot_nt, split(d_ref[HALF:, :HALF]), split(w1_ref[...]))
            d_ref[HALF:, :HALF] = low
            parts = split(low)
            s_ref[...] = d_ref[HALF:, HALF:] - dot3(dot_nt, parts, parts)

        invert_factor(s_ref, w2_ref)

        @pl.when(odd == 0)
        def _():
            w1_ref[...] = w2_ref[...]

        for static in range(STEPS):

            @pl.when((k == static) & (odd == 1))
            def _():
                first = split(w1_ref[...])
                second = split(w2_ref[...])
                corner = dot3(dot_nn, split(d_ref[HALF:, :HALF]), first)
                corner = split(-dot3(dot_nn, second, split(corner)))
                for part, w_ref in enumerate((wh_ref, wl_ref)):
                    w_ref[static, :HALF, :HALF] = first[part]
                    w_ref[static, :HALF, HALF:] = jnp.zeros((HALF, HALF), bf16)
                    w_ref[static, HALF:, :HALF] = corner[part]
                    w_ref[static, HALF:, HALF:] = second[part]

                @pl.loop(static + 1, STEPS)
                def _(tile):
                    rows = pl.ds(pl.multiple_of(tile * WIDE, WIDE), WIDE)
                    here = pl.ds(static * WIDE, WIDE)
                    block = a_ref[rows, here]
                    if static:
                        block = block - earlier(static, rows)
                    low = split(dot3(dot_nt, split(block), (wh_ref[static], wl_ref[static])))
                    lh_ref[rows, here] = low[0]
                    ll_ref[rows, here] = low[1]

                if static < STEPS - 1:
                    for which in range(2):
                        leave(static, which).start()

        return carry

    lax.fori_loop(0, 2 * STEPS, half, 0)
    for k in range(STEPS - 1):
        for which in range(2):
            leave(k, which).wait()


def factor_tile(tile):
    wide = jax.ShapeDtypeStruct((ORDER, ORDER), bf16)
    inverse = jax.ShapeDtypeStruct((STEPS, WIDE, WIDE), bf16)
    return pl.pallas_call(
        factor_kernel,
        out_shape=(wide, wide, inverse, inverse),
        in_specs=[pl.BlockSpec(memory_space=pl.ANY)],
        out_specs=(
            pl.BlockSpec(memory_space=pl.ANY),
            pl.BlockSpec(memory_space=pl.ANY),
            pl.BlockSpec(memory_space=pltpu.VMEM),
            pl.BlockSpec(memory_space=pltpu.VMEM),
        ),
        scratch_shapes=[
            pltpu.VMEM((ORDER, ORDER), f32),
            pltpu.VMEM((ORDER, ORDER), bf16),
            pltpu.VMEM((ORDER, ORDER), bf16),
            pltpu.VMEM((WIDE, WIDE), f32),
            pltpu.VMEM((HALF, HALF), f32),
            pltpu.VMEM((HALF, HALF), f32),
            pltpu.VMEM((HALF, HALF), f32),
            pltpu.SemaphoreType.DMA((STEPS,)),
            pltpu.SemaphoreType.DMA((2, STEPS)),
        ],
        compiler_params=pltpu.CompilerParams(vmem_limit_bytes=56 * 2**20),
        cost_estimate=pl.CostEstimate(flops=60 * 10**9, bytes_accessed=32 * 2**20, transcendentals=0),
    )(tile)


def update_kernel(
    ri_ref, rj_ref, lh_hbm, ll_hbm, wh_ref, wl_ref, left_ref, vi_ref, vj_ref, out_ref, solved_ref,
    lh_ref, ll_ref, xh_ref, xl_ref, sem,
):
    def arrive(k, which):
        at = pl.ds(k * WIDE, WIDE)
        source, target = ((lh_hbm, lh_ref), (ll_hbm, ll_ref))[which]
        return pltpu.make_async_copy(
            source.at[at, pl.ds(0, k * WIDE)], target.at[at, pl.ds(0, k * WIDE)], sem.at[which, k]
        )

    for k in range(1, STEPS):
        for which in range(2):
            arrive(k, which).start()

    column = lax.broadcasted_iota(jnp.int32, (WIDE, WIDE), 1)
    sources = ((vi_ref, ri_ref), (vj_ref, rj_ref))
    for k in range(STEPS):
        here = pl.ds(k * WIDE, WIDE)
        done = pl.ds(0, k * WIDE)
        if k:
            for which in range(2):
                arrive(k, which).wait()
        for side, (v_ref, rank_ref) in enumerate(sources):
            at = pl.ds(side * WIDE, WIDE)
            block = jnp.where(column < rank_ref[0], v_ref[here, :].astype(f32), 0.0)
            if k:
                block = block - dot3(
                    dot_nn, (lh_ref[here, done], ll_ref[here, done]), (xh_ref[done, at], xl_ref[done, at])
                )
            solved = split(dot3(dot_nn, (wh_ref[k], wl_ref[k]), split(block)))
            xh_ref[here, at] = solved[0]
            xl_ref[here, at] = solved[1]

    core = dot_tn(xh_ref[:, :WIDE], xh_ref[:, WIDE:]).astype(bf16)
    width = solved_ref.shape[1]
    pick = lax.broadcasted_iota(jnp.int32, (WIDE, width), 0) == (
        lax.axis_index("col") * width + lax.broadcasted_iota(jnp.int32, (WIDE, width), 1)
    )
    pick = pick.astype(bf16)
    for k in range(STEPS):
        here = pl.ds(k * WIDE, WIDE)
        left = left_ref[here, :]
        left = jnp.where(column < ri_ref[0], left, jnp.zeros_like(left))
        out_ref[here, :] = (-dot_nn(left, core)).astype(bf16)
        solved_ref[here, :] = dot_nn(xh_ref[here, :WIDE], pick).astype(bf16)


def update_tiles(rows_rank, cols_rank, factor, left, right_i, right_j, width):
    scalar = pl.BlockSpec(memory_space=pltpu.SMEM)
    anywhere = pl.BlockSpec(memory_space=pl.ANY)
    vmem = pl.BlockSpec(memory_space=pltpu.VMEM)
    return pl.pallas_call(
        update_kernel,
        out_shape=(jax.ShapeDtypeStruct((ORDER, WIDE), bf16), jax.ShapeDtypeStruct((ORDER, width), bf16)),
        in_specs=[scalar, scalar, anywhere, anywhere, vmem, vmem, vmem, vmem, vmem],
        out_specs=(vmem, vmem),
        scratch_shapes=[
            pltpu.VMEM((ORDER, ORDER), bf16),
            pltpu.VMEM((ORDER, ORDER), bf16),
            pltpu.VMEM((ORDER, 2 * WIDE), bf16),
            pltpu.VMEM((ORDER, 2 * WIDE), bf16),
            pltpu.SemaphoreType.DMA((2, STEPS)),
        ],
        compiler_params=pltpu.CompilerParams(vmem_limit_bytes=56 * 2**20),
        cost_estimate=pl.CostEstimate(flops=10 * 10**9, bytes_accessed=32 * 2**20, transcendentals=0),
    )(rows_rank, cols_rank, *factor, left, right_i, right_j)


def local(diag_tile, rows_left, rows_right, rows_rank, cols_right, cols_rank):
    partial_value = lax.all_gather(diag_tile, "col", axis=1, tiled=True)
    whole_tile = lax.all_gather(partial_value, "row", axis=0, tiled=True)
    left = lax.all_gather(rows_left[0], "col", axis=1, tiled=True)
    right_i = lax.all_gather(rows_right[0], "col", axis=1, tiled=True)
    right_j = lax.all_gather(cols_right[0], "row", axis=1, tiled=True)
    factor = factor_tile(whole_tile)
    update, solved = update_tiles(rows_rank, cols_rank, factor, left, right_i, right_j, rows_right.shape[2])
    return update[None, None], solved[None]


def solution(mesh):
    placed = (
        P("row", "col"),
        P("row", None, "col"),
        P("row", None, "col"),
        P("row"),
        P("col", None, "row"),
        P("col"),
    )
    return jax.shard_map(
        local,
        mesh=mesh,
        in_specs=placed,
        out_specs=(P("row", "col", None, None), P("row", None, "col")),
        check_vma=False,
    )
```

```python
import functools

import jax
import jax.numpy as jnp
from jax import lax
from jax.experimental import pallas as pl
from jax.experimental.pallas import tpu as pltpu
from jax.sharding import PartitionSpec as P

f32 = jnp.float32
bf16 = jnp.bfloat16
ORDER = 2048
WIDE = 256
HALF = 128
STEPS = ORDER // WIDE
SLABS = 4
PIECE = 16
MESH = pl.DeviceIdType.MESH


def split(x):
    high = x.astype(bf16)
    return high, (x - high.astype(f32)).astype(bf16)


def dot_nt(a, b):
    return lax.dot_general(a, b, (((1,), (1,)), ((), ())), preferred_element_type=f32)


def dot_nn(a, b):
    return lax.dot_general(a, b, (((1,), (0,)), ((), ())), preferred_element_type=f32)


def dot_tn(a, b):
    return lax.dot_general(a, b, (((0,), (0,)), ((), ())), preferred_element_type=f32)


def dot3(dot, a, b):
    return dot(a[0], b[0]) + (dot(a[0], b[1]) + dot(a[1], b[0]))


def invert_factor(s_ref, w_ref):
    lane = lax.broadcasted_iota(jnp.int32, (8, HALF), 1)
    sub = lax.broadcasted_iota(jnp.int32, (8, HALF), 0)
    for group in range(HALF // 8):
        first = 8 * group
        rows = s_ref[first : first + 8, :]
        in_group = (lane >= first) & (lane < first + 8)
        columns = [jnp.broadcast_to(rows[:, first + c : first + c + 1], (8, HALF)) for c in range(8)]
        g = {}
        for c in range(8):
            for r in range(c + 1):
                g[r, c] = jnp.broadcast_to(columns[c][r : r + 1, :], (8, HALF))
        inverse = []
        factor = {}
        for k in range(8):
            inverse.append(1.0 / g[k, k])
            for c in range(k + 1, 8):
                factor[k, c] = g[k, c] * inverse[k]
            for r in range(k + 1, 8):
                for c in range(r, 8):
                    g[r, c] = g[r, c] - factor[k, r] * g[k, c]
        start = jnp.where(in_group, (lane - first == sub).astype(f32), rows)
        pivot_rows = []
        for k in range(8):
            row = jnp.broadcast_to(start[k : k + 1, :], (8, HALF))
            for j in range(k):
                row = row - factor[j, k] * pivot_rows[j]
            pivot_rows.append(row)
        done = jnp.zeros((8, HALF), f32)
        for k in range(8):
            done = jnp.where(sub == k, pivot_rows[k] * lax.rsqrt(g[k, k]), done)
        w_ref[first : first + 8, :] = jnp.where(lane - first <= sub, done, 0.0)
        for below in range(group + 1, HALF // 8):
            block = s_ref[8 * below : 8 * below + 8, :]
            m = []
            for c in range(8):
                value = jnp.broadcast_to(block[:, first + c : first + c + 1], (8, HALF))
                for j in range(c):
                    value = value - m[j] * g[j, c]
                m.append(value * inverse[c])
            block = jnp.where(in_group, 0.0, block)
            for c in range(8):
                block = block - m[c] * pivot_rows[c]
            s_ref[8 * below : 8 * below + 8, :] = block


def panel_kernel(
    ri_ref, rj_ref, diag_ref, left_ref, vi_ref, vj_ref, out_ref, solved_ref,
    a_ref, uv_ref, vj_all, lh_ref, ll_ref, wh_ref, wl_ref, d_ref, s_ref, w1_ref, w2_ref,
    first_send, first_recv, y_send, y_recv, z_send, z_recv, x_send, x_recv, c_send, c_recv,
    ux_send, ux_recv, uc_sem, jz_send, jz_recv, jy_send, jy_recv,
):
    row = lax.axis_index("row")
    col = lax.axis_index("col")
    y, z = row // 8, row % 8
    x, core = col // 2, col % 2
    sibling = (row, col + 1 - 2 * core)

    def along_x(d):
        return (x + d) % 4

    def along_y(d):
        return (y + d) % 4

    def along_z(d):
        return (z + d) % 8

    def at_x(to):
        return (row, 2 * to + core)

    def at_y(to):
        return (8 * to + z, col)

    def at_z(to):
        return (8 * y + to, col)

    def send(part, send_sem, recv_sem, device):
        return pltpu.make_async_remote_copy(
            src_ref=part, dst_ref=part, send_sem=send_sem, recv_sem=recv_sem, device_id=device, device_id_type=MESH
        )

    def first_copy(d):
        to = along_x(d)
        return pltpu.make_async_remote_copy(
            src_ref=diag_ref.at[pl.ds(PIECE * to, PIECE)],
            dst_ref=a_ref.at[core, x, row, pl.ds(PIECE * to, PIECE)],
            send_sem=first_send.at[d - 1],
            recv_sem=first_recv.at[x],
            device_id=at_x(to),
            device_id_type=MESH,
        )

    def y_copy(slab, d):
        part = a_ref.at[core, pl.ds(0, slab + 1), row, pl.ds(PIECE * x, PIECE)]
        return send(part, y_send.at[d - 1], y_recv.at[slab], at_y(along_y(d)))

    def z_copy(slab, d):
        part = a_ref.at[core, pl.ds(0, slab + 1), 8 * slab + z, pl.ds(PIECE * x, PIECE)]
        return send(part, z_send.at[slab, d - 1], z_recv.at[slab, z], at_z(along_z(d)))

    def x_copy(slab, d):
        part = a_ref.at[core, pl.ds(0, slab + 1), pl.ds(8 * slab, 8), pl.ds(PIECE * x, PIECE)]
        return send(part, x_send.at[slab, d - 1], x_recv.at[slab, x], at_x(along_x(d)))

    def c_copy(slab):
        part = a_ref.at[core, pl.ds(0, slab + 1), pl.ds(8 * slab, 8)]
        return send(part, c_send.at[slab], c_recv.at[slab], sibling)

    def first_stage():
        @pl.when(x <= y)
        def _():
            for d in range(1, 4):
                first_copy(d).start()
            own = pl.ds(pl.multiple_of(PIECE * x, PIECE), PIECE)
            a_ref[core, x, row, own] = diag_ref[own, :]

    def y_stage():
        for source in range(4):
            @pl.when((source <= y) & (source != x))
            def _():
                part = a_ref.at[core, source, row, pl.ds(PIECE * x, PIECE)]
                send(part, first_send.at[0], first_recv.at[source], sibling).wait_recv()

        for slab in range(SLABS):
            @pl.when(y == slab)
            def _():
                for d in range(1, 4):
                    y_copy(slab, d).start()

    def z_stage(slab):
        @pl.when(y != slab)
        def _():
            part = a_ref.at[core, pl.ds(0, slab + 1), 8 * slab + z, pl.ds(PIECE * x, PIECE)]
            send(part, y_send.at[0], y_recv.at[slab], sibling).wait_recv()

        for d in range(1, 8):
            z_copy(slab, d).start()

    def x_stage(slab):
        for d in range(1, 8):
            source = along_z(d)
            part = a_ref.at[core, pl.ds(0, slab + 1), 8 * slab + source, pl.ds(PIECE * x, PIECE)]
            send(part, z_send.at[slab, 0], z_recv.at[slab, source], sibling).wait_recv()
        for d in range(1, 4):
            x_copy(slab, d).start()

    def c_stage(slab):
        for d in range(1, 4):
            source = along_x(d)
            part = a_ref.at[core, pl.ds(0, slab + 1), pl.ds(8 * slab, 8), pl.ds(PIECE * source, PIECE)]
            send(part, x_send.at[slab, 0], x_recv.at[slab, source], sibling).wait_recv()
        c_copy(slab).start()

    def ready(slab):
        part = a_ref.at[1 - core, pl.ds(0, slab + 1), pl.ds(8 * slab, 8)]
        send(part, c_send.at[slab], c_recv.at[slab], sibling).wait_recv()

    def ux_copy(d):
        return send(uv_ref.at[core, x], ux_send.at[d - 1], ux_recv.at[x], at_x(along_x(d)))

    def uc_copy():
        return send(uv_ref.at[core], uc_sem.at[0], uc_sem.at[1], sibling)

    def jz_copy(d):
        return send(vj_all.at[y, z], jz_send.at[d - 1], jz_recv.at[z], at_z(along_z(d)))

    def jy_copy(d):
        return send(vj_all.at[y], jy_send.at[d - 1], jy_recv.at[y], at_y(along_y(d)))

    def factors_first():
        for d in range(1, 8):
            jz_copy(d).start()
        for d in range(1, 4):
            ux_copy(d).start()

    def factors_second():
        for d in range(1, 8):
            source = along_z(d)
            send(vj_all.at[y, source], jz_send.at[0], jz_recv.at[source], sibling).wait_recv()
        for d in range(1, 4):
            jy_copy(d).start()
        for d in range(1, 4):
            source = along_x(d)
            send(uv_ref.at[core, source], ux_send.at[0], ux_recv.at[source], sibling).wait_recv()
        uc_copy().start()

    def factors_ready():
        for d in range(1, 4):
            source = along_y(d)
            send(vj_all.at[source], jy_send.at[0], jy_recv.at[source], sibling).wait_recv()
        send(uv_ref.at[1 - core], uc_sem.at[0], uc_sem.at[1], sibling).wait_recv()

    def wait_sends():
        @pl.when(x <= y)
        def _():
            for d in range(1, 4):
                first_copy(d).wait_send()

        for slab in range(SLABS):
            @pl.when(y == slab)
            def _():
                for d in range(1, 4):
                    y_copy(slab, d).wait_send()

            for d in range(1, 8):
                z_copy(slab, d).wait_send()
            for d in range(1, 4):
                x_copy(slab, d).wait_send()
            c_copy(slab).wait_send()
        for d in range(1, 8):
            jz_copy(d).wait_send()
        for d in range(1, 4):
            jy_copy(d).wait_send()
            ux_copy(d).wait_send()
        uc_copy().wait_send()

    barrier = pltpu.get_barrier_semaphore()
    partners = [sibling]
    partners += [at_x(along_x(d)) for d in range(1, 4)]
    partners += [at_y(along_y(d)) for d in range(1, 4)]
    partners += [at_z(along_z(d)) for d in range(1, 8)]
    for device in partners:
        pl.semaphore_signal(barrier, inc=1, device_id=device, device_id_type=MESH)
    pl.semaphore_wait(barrier, len(partners))

    first_stage()
    uv_ref[core, x, 0] = left_ref[...]
    uv_ref[core, x, 1] = vi_ref[...]
    own = vj_ref[...].astype(f32)
    vj_all[y, z] = jnp.concatenate([own[:, : ORDER // 2], own[:, ORDER // 2 :]], axis=0).astype(bf16)
    y_stage()
    z_stage(0)
    x_stage(0)
    z_stage(1)
    c_stage(0)
    ready(0)

    schedule = {
        1: lambda: (x_stage(1), z_stage(2)),
        2: lambda: (c_stage(1), x_stage(2)),
        3: lambda: (z_stage(3),),
        4: lambda: (ready(1), c_stage(2), factors_first()),
        5: lambda: (x_stage(3),),
        6: lambda: (factors_second(),),
        7: lambda: (c_stage(3),),
        8: lambda: (ready(2),),
        12: lambda: (ready(3),),
    }

    def tile_of(k, j):
        return a_ref[j % 2, j // 2, 4 * k : 4 * k + 4].reshape(WIDE, WIDE)

    def solve_tile(block, rows, j):
        here = pl.ds(j * WIDE, WIDE)
        done = pl.ds(0, j * WIDE)
        if j:
            block = block - dot3(
                dot_nt, (lh_ref[rows, done], ll_ref[rows, done]), (lh_ref[here, done], ll_ref[here, done])
            )
        low = split(dot3(dot_nt, split(block), (wh_ref[j], wl_ref[j])))
        lh_ref[rows, here] = low[0]
        ll_ref[rows, here] = low[1]

    def half(h, carry):
        k = h // 2
        odd = h % 2

        for step, act in schedule.items():
            pl.when(h == step)(lambda act=act: (act(), None)[1])

        for static in range(STEPS):

            @pl.when((k == static) & (odd == 0))
            def _():
                here = pl.ds(static * WIDE, WIDE)
                done = pl.ds(0, static * WIDE)
                for j in range(static):
                    solve_tile(tile_of(static, j), here, j)
                block = tile_of(static, static)
                if static:
                    parts = (lh_ref[here, done], ll_ref[here, done])
                    block = block - dot3(dot_nt, parts, parts)
                d_ref[...] = block
                s_ref[...] = block[:HALF, :HALF]

        @pl.when(odd == 1)
        def _():
            low = dot3(dot_nt, split(d_ref[HALF:, :HALF]), split(w1_ref[...]))
            d_ref[HALF:, :HALF] = low
            parts = split(low)
            s_ref[...] = d_ref[HALF:, HALF:] - dot3(dot_nt, parts, parts)

        invert_factor(s_ref, w2_ref)

        @pl.when(odd == 0)
        def _():
            w1_ref[...] = w2_ref[...]

        @pl.when(odd == 1)
        def _():
            first = split(w1_ref[...])
            second = split(w2_ref[...])
            corner = dot3(dot_nn, split(d_ref[HALF:, :HALF]), first)
            corner = split(-dot3(dot_nn, second, split(corner)))
            for part, w_ref in enumerate((wh_ref, wl_ref)):
                w_ref[k, :HALF, :HALF] = first[part]
                w_ref[k, :HALF, HALF:] = jnp.zeros((HALF, HALF), bf16)
                w_ref[k, HALF:, :HALF] = corner[part]
                w_ref[k, HALF:, HALF:] = second[part]

        return carry

    lax.fori_loop(0, 2 * STEPS, half, 0)

    factors_ready()
    column = lax.broadcasted_iota(jnp.int32, (WIDE, WIDE), 0)
    rows_i = pl.ds(ORDER, WIDE)
    rows_j = pl.ds(ORDER + WIDE, WIDE)
    for j in range(STEPS):
        at = pl.ds(j * WIDE, WIDE)
        tile = jnp.concatenate([uv_ref[c % 2, c // 2, 1, :, at] for c in range(8)], axis=0).astype(f32)
        solve_tile(jnp.where(column < ri_ref[0], tile, 0.0), rows_i, j)
        at = pl.ds((j % 4) * WIDE, WIDE)
        tile = vj_all[:, :, :, at].astype(f32)[:, :, 8 * (j // 4) : 8 * (j // 4) + 8].reshape(WIDE, WIDE)
        solve_tile(jnp.where(column < rj_ref[0], tile, 0.0), rows_j, j)

    product = dot_nt(lh_ref[rows_i, :], lh_ref[rows_j, :]).astype(bf16)
    width = solved_ref.shape[0]
    solved_ref[...] = lh_ref[pl.ds(pl.multiple_of(ORDER + col * width, width), width), :]
    for j in range(STEPS):
        at = pl.ds(j * WIDE, WIDE)
        left = jnp.concatenate([uv_ref[c % 2, c // 2, 0, :, at] for c in range(8)], axis=0)
        left = jnp.where(column < ri_ref[0], left, jnp.zeros_like(left))
        out_ref[at, :] = (-dot_tn(left, product)).astype(bf16)
    wait_sends()


def update_panel(rows_rank, cols_rank, diag_tile, left, right_i, right_j):
    scalar = pl.BlockSpec(memory_space=pltpu.SMEM)
    vmem = pl.BlockSpec(memory_space=pltpu.VMEM)
    dma = pltpu.SemaphoreType.DMA
    return pl.pallas_call(
        panel_kernel,
        out_shape=(jax.ShapeDtypeStruct((ORDER, WIDE), bf16), jax.ShapeDtypeStruct(right_i.shape, bf16)),
        in_specs=[scalar, scalar, vmem, vmem, vmem, vmem],
        out_specs=(vmem, vmem),
        scratch_shapes=[
            pltpu.VMEM((2, 4, 32, 64, WIDE), f32),
            pltpu.VMEM((2, 4, 2, 32, ORDER), bf16),
            pltpu.VMEM((4, 8, 16, ORDER // 2), bf16),
            pltpu.VMEM((ORDER + 2 * WIDE, ORDER), bf16),
            pltpu.VMEM((ORDER + 2 * WIDE, ORDER), bf16),
            pltpu.VMEM((STEPS, WIDE, WIDE), bf16),
            pltpu.VMEM((STEPS, WIDE, WIDE), bf16),
            pltpu.VMEM((WIDE, WIDE), f32),
            pltpu.VMEM((HALF, HALF), f32),
            pltpu.VMEM((HALF, HALF), f32),
            pltpu.VMEM((HALF, HALF), f32),
            dma((3,)), dma((4,)), dma((3,)), dma((4,)),
            dma((4, 7)), dma((4, 8)), dma((4, 3)), dma((4, 4)), dma((4,)), dma((4,)),
            dma((3,)), dma((4,)), dma((2,)), dma((7,)), dma((8,)), dma((3,)), dma((4,)),
        ],
        compiler_params=pltpu.CompilerParams(
            collective_id=0, has_side_effects=True, vmem_limit_bytes=58 * 2**20
        ),
    )(rows_rank, cols_rank, diag_tile, left, right_i, right_j)


def local(diag_tile, rows_left, rows_right, rows_rank, cols_right, cols_rank):
    update, solved = update_panel(
        rows_rank, cols_rank, diag_tile, rows_left[0].T, rows_right[0].T, cols_right[0].T
    )
    return update[None, None], solved.T[None]


def solution(mesh):
    placed = (
        P("row", "col"),
        P("row", None, "col"),
        P("row", None, "col"),
        P("row"),
        P("col", None, "row"),
        P("col"),
    )
    return jax.shard_map(
        local,
        mesh=mesh,
        in_specs=placed,
        out_specs=(P("row", "col", None, None), P("row", None, "col")),
        check_vma=False,
    )
```

```python
import functools

import jax
import jax.numpy as jnp
from jax import lax
from jax.experimental import pallas as pl
from jax.experimental.pallas import tpu as pltpu
from jax.sharding import PartitionSpec as P

f32 = jnp.float32
bf16 = jnp.bfloat16
ORDER = 2048
WIDE = 256
HALF = 128
STEPS = ORDER // WIDE
SLABS = 4
PIECE = 16
MESH = pl.DeviceIdType.MESH


def split(x):
    high = x.astype(bf16)
    return high, (x - high.astype(f32)).astype(bf16)


def dot_nt(a, b):
    return lax.dot_general(a, b, (((1,), (1,)), ((), ())), preferred_element_type=f32)


def dot_nn(a, b):
    return lax.dot_general(a, b, (((1,), (0,)), ((), ())), preferred_element_type=f32)


def dot_tn(a, b):
    return lax.dot_general(a, b, (((0,), (0,)), ((), ())), preferred_element_type=f32)


def dot3(dot, a, b):
    return dot(a[0], b[0]) + (dot(a[0], b[1]) + dot(a[1], b[0]))


def invert_factor(s_ref, w_ref, job=None):
    lane = lax.broadcasted_iota(jnp.int32, (8, HALF), 1)
    sub = lax.broadcasted_iota(jnp.int32, (8, HALF), 0)
    count = HALF // 8

    def spread(block, first):
        return [jnp.broadcast_to(block[:, first + c : first + c + 1], (8, HALF)) for c in range(8)]

    def one(value, r):
        return jnp.broadcast_to(value[r : r + 1, :], (8, HALF))

    diag = spread(s_ref[0:8, :], 0)
    under = spread(s_ref[8:16, :], 0)
    for group in range(count):
        first = 8 * group
        in_group = (lane >= first) & (lane < first + 8)
        rows = s_ref[first : first + 8, :]
        blocks = {q: s_ref[8 * q : 8 * q + 8, :] for q in range(group + 1, count)}
        if group + 1 < count:
            next_diag = spread(blocks[group + 1], first + 8)
        if group + 2 < count:
            next_under = spread(blocks[group + 2], first + 8)
        g = {}
        for c in range(8):
            for r in range(c + 1):
                g[r, c] = one(diag[c], r)
        inverse = []
        factor = {}
        for k in range(8):
            inverse.append(1.0 / g[k, k])
            for c in range(k + 1, 8):
                factor[k, c] = g[k, c] * inverse[k]
            for r in range(k + 1, 8):
                for c in range(r, 8):
                    g[r, c] = g[r, c] - factor[k, r] * g[k, c]

        def multipliers(columns):
            values, m = [], []
            for c in range(8):
                value = columns[c]
                for j in range(c):
                    value = value - m[j] * g[j, c]
                values.append(value)
                m.append(value * inverse[c])
            return values, m

        m_of = {}
        if group + 1 < count:
            values, m_of[group + 1] = multipliers(under)
            for c in range(8):
                for k in range(8):
                    pivot = one(values[k], c)
                    next_diag[c] = next_diag[c] - m_of[group + 1][k] * pivot
                    if group + 2 < count:
                        if k == 0 and c == 0:
                            m_of[group + 2] = multipliers(spread(blocks[group + 2], first))[1]
                        next_under[c] = next_under[c] - m_of[group + 2][k] * pivot
            diag = next_diag
            if group + 2 < count:
                under = next_under
        start = jnp.where(in_group, (lane - first == sub).astype(f32), rows)
        pivot_rows = []
        for k in range(8):
            row = one(start, k)
            for j in range(k):
                row = row - factor[j, k] * pivot_rows[j]
            pivot_rows.append(row)
        done = jnp.zeros((8, HALF), f32)
        for k in range(8):
            done = jnp.where(sub == k, pivot_rows[k] * lax.rsqrt(g[k, k]), done)
        w_ref[first : first + 8, :] = jnp.where(lane - first <= sub, done, 0.0)
        reduced = list(pivot_rows)
        if group + 3 < count:
            for k in reversed(range(8)):
                for j in range(k + 1, 8):
                    reduced[k] = reduced[k] - g[k, j] * reduced[j]
                reduced[k] = reduced[k] * inverse[k]
        for q, block in blocks.items():
            by = m_of[q] if q in m_of else spread(block, first)
            of = pivot_rows if q in m_of else reduced
            block = jnp.where(in_group, 0.0, block)
            for c in range(8):
                block = block - by[c] * of[c]
            s_ref[8 * q : 8 * q + 8, :] = block
        if job is not None:
            job(group)


def panel_kernel(
    ri_ref, rj_ref, diag_ref, left_ref, vi_ref, vj_ref, out_ref, solved_ref,
    a_ref, uv_ref, vj_all, lh_ref, ll_ref, wh_ref, wl_ref, d_ref, s_ref, w1_ref, w2_ref, total_ref,
    first_send, first_recv, y_send, y_recv, z_send, z_recv, x_send, x_recv, c_send, c_recv,
    ux_send, ux_recv, uc_sem, jz_send, jz_recv, jy_send, jy_recv,
):
    row = lax.axis_index("row")
    col = lax.axis_index("col")
    y, z = row // 8, row % 8
    x, core = col // 2, col % 2
    sibling = (row, col + 1 - 2 * core)

    def along_x(d):
        return (x + d) % 4

    def along_y(d):
        return (y + d) % 4

    def along_z(d):
        return (z + d) % 8

    def at_x(to):
        return (row, 2 * to + core)

    def at_y(to):
        return (8 * to + z, col)

    def at_z(to):
        return (8 * y + to, col)

    def send(part, send_sem, recv_sem, device):
        return pltpu.make_async_remote_copy(
            src_ref=part, dst_ref=part, send_sem=send_sem, recv_sem=recv_sem, device_id=device, device_id_type=MESH
        )

    def deal_copy(d):
        to = jnp.where(core == 0, along_x(d), along_y(d))
        device = (jnp.where(core == 0, row, 8 * along_y(d) + z), jnp.where(core == 0, 2 * along_x(d), col))
        return pltpu.make_async_remote_copy(
            src_ref=diag_ref.at[pl.ds(PIECE * to, PIECE)],
            dst_ref=a_ref.at[core, x, row, pl.ds(PIECE * to, PIECE)],
            send_sem=first_send.at[d - 1],
            recv_sem=first_recv.at[jnp.where(core == 0, x, y)],
            device_id=device,
            device_id_type=MESH,
        )

    def mine(slab):
        return pl.ds(PIECE * jnp.where(core == 0, x, y), PIECE)

    def rows_part(slab, source, columns=None):
        columns = pl.ds(0, slab + 1) if columns is None else columns
        return a_ref.at[core, columns, 8 * slab + source, mine(slab)]

    def spread_copy(slab, d):
        return send(rows_part(slab, z), y_send.at[slab, d - 1], y_recv.at[slab, 0], at_y(along_y(d)))

    def spread_column(slab, d):
        return send(rows_part(slab, z, x), y_send.at[slab, d - 1], y_recv.at[slab, x], at_x(along_x(d)))

    def z_copy(slab, d):
        return send(rows_part(slab, z), z_send.at[slab, d - 1], z_recv.at[slab, z], at_z(along_z(d)))

    def last_part(slab, source):
        return a_ref.at[core, pl.ds(0, slab + 1), pl.ds(8 * slab, 8), pl.ds(PIECE * source, PIECE)]

    def last_copy(slab, d):
        at = jnp.where(core == 0, x, y)
        device = (jnp.where(core == 0, row, 8 * along_y(d) + z), jnp.where(core == 0, 2 * along_x(d), col))
        return send(last_part(slab, at), x_send.at[slab, d - 1], x_recv.at[slab, at], device)

    def c_copy(slab):
        part = a_ref.at[core, pl.ds(0, slab + 1), pl.ds(8 * slab, 8)]
        return send(part, c_send.at[slab], c_recv.at[slab], sibling)

    def first_stage():
        @pl.when(x <= y)
        def _():
            for d in range(1, 4):
                deal_copy(d).start()
            own = pl.ds(pl.multiple_of(PIECE * jnp.where(core == 0, x, y), PIECE), PIECE)
            a_ref[core, x, row, own] = diag_ref[own, :]

    def spread_stage():
        @pl.when(core == 0)
        def _():
            for source in range(4):
                @pl.when((source <= y) & (source != x))
                def _():
                    part = a_ref.at[core, source, row, mine(0)]
                    send(part, first_send.at[0], first_recv.at[source], sibling).wait_recv()

            for slab in range(SLABS):
                @pl.when(y == slab)
                def _():
                    for d in range(1, 4):
                        spread_copy(slab, d).start()

        @pl.when(core == 1)
        def _():
            for slab in range(SLABS):
                @pl.when((x <= slab) & (slab != y))
                def _():
                    send(rows_part(slab, z, x), first_send.at[0], first_recv.at[slab], sibling).wait_recv()

                @pl.when(x <= slab)
                def _():
                    for d in range(1, 4):
                        spread_column(slab, d).start()

    def z_stage(slab):
        @pl.when((core == 0) & (y != slab))
        def _():
            send(rows_part(slab, z), y_send.at[0, 0], y_recv.at[slab, 0], sibling).wait_recv()

        for source in range(slab + 1):
            @pl.when((core == 1) & (x != source))
            def _():
                send(rows_part(slab, z, source), y_send.at[0, 0], y_recv.at[slab, source], sibling).wait_recv()

        for d in range(1, 8):
            z_copy(slab, d).start()

    def last_stage(slab):
        for d in range(1, 8):
            source = along_z(d)
            send(rows_part(slab, source), z_send.at[slab, 0], z_recv.at[slab, source], sibling).wait_recv()
        for d in range(1, 4):
            last_copy(slab, d).start()

    def c_stage(slab):
        for d in range(1, 4):
            source = jnp.where(core == 0, along_x(d), along_y(d))
            send(last_part(slab, source), x_send.at[slab, 0], x_recv.at[slab, source], sibling).wait_recv()
        c_copy(slab).start()

    def ready(slab):
        part = a_ref.at[1 - core, pl.ds(0, slab + 1), pl.ds(8 * slab, 8)]
        send(part, c_send.at[slab], c_recv.at[slab], sibling).wait_recv()

    def ux_copy(d):
        return send(uv_ref.at[core, x], ux_send.at[d - 1], ux_recv.at[x], at_x(along_x(d)))

    def uc_copy():
        return send(uv_ref.at[core], uc_sem.at[0], uc_sem.at[1], sibling)

    def jz_copy(d):
        return send(vj_all.at[y, z], jz_send.at[d - 1], jz_recv.at[z], at_z(along_z(d)))

    def jy_copy(d):
        return send(vj_all.at[y], jy_send.at[d - 1], jy_recv.at[y], at_y(along_y(d)))

    def factors_first():
        for d in range(1, 8):
            jz_copy(d).start()
        for d in range(1, 4):
            ux_copy(d).start()

    def factors_second():
        for d in range(1, 8):
            source = along_z(d)
            send(vj_all.at[y, source], jz_send.at[0], jz_recv.at[source], sibling).wait_recv()
        for d in range(1, 4):
            jy_copy(d).start()
        for d in range(1, 4):
            source = along_x(d)
            send(uv_ref.at[core, source], ux_send.at[0], ux_recv.at[source], sibling).wait_recv()
        uc_copy().start()

    def factors_ready():
        for d in range(1, 4):
            source = along_y(d)
            send(vj_all.at[source], jy_send.at[0], jy_recv.at[source], sibling).wait_recv()
        send(uv_ref.at[1 - core], uc_sem.at[0], uc_sem.at[1], sibling).wait_recv()

    def wait_sends():
        @pl.when(x <= y)
        def _():
            for d in range(1, 4):
                deal_copy(d).wait_send()

        for slab in range(SLABS):
            @pl.when((core == 0) & (y == slab))
            def _():
                for d in range(1, 4):
                    spread_copy(slab, d).wait_send()

            @pl.when((core == 1) & (x <= slab))
            def _():
                for d in range(1, 4):
                    spread_column(slab, d).wait_send()

            for d in range(1, 8):
                z_copy(slab, d).wait_send()
            for d in range(1, 4):
                last_copy(slab, d).wait_send()
            c_copy(slab).wait_send()
        for d in range(1, 8):
            jz_copy(d).wait_send()
        for d in range(1, 4):
            jy_copy(d).wait_send()
            ux_copy(d).wait_send()
        uc_copy().wait_send()

    barrier = pltpu.get_barrier_semaphore()
    partners = [sibling]
    partners += [at_x(along_x(d)) for d in range(1, 4)]
    partners += [at_y(along_y(d)) for d in range(1, 4)]
    partners += [at_z(along_z(d)) for d in range(1, 8)]
    for device in partners:
        pl.semaphore_signal(barrier, inc=1, device_id=device, device_id_type=MESH)

    @pl.loop(0, lh_ref.shape[0] // WIDE)
    def _(tile):
        rows = pl.ds(pl.multiple_of(tile * WIDE, WIDE), WIDE)
        lh_ref[rows, :] = jnp.zeros((WIDE, ORDER), bf16)
        ll_ref[rows, :] = jnp.zeros((WIDE, ORDER), bf16)

    pl.semaphore_wait(barrier, len(partners))

    first_stage()
    uv_ref[core, x, 0] = left_ref[...]
    uv_ref[core, x, 1] = vi_ref[...]
    own = vj_ref[...].astype(f32)
    vj_all[y, z] = jnp.concatenate([own[:, : ORDER // 2], own[:, ORDER // 2 :]], axis=0).astype(bf16)
    spread_stage()
    z_stage(0)
    z_stage(1)
    last_stage(0)
    c_stage(0)
    ready(0)

    schedule = {
        1: lambda: (last_stage(1), z_stage(2)),
        2: lambda: (c_stage(1),),
        3: lambda: (last_stage(2), z_stage(3)),
        4: lambda: (ready(1), factors_first()),
        5: lambda: (c_stage(2), last_stage(3)),
        7: lambda: (factors_second(),),
        8: lambda: (ready(2), factors_ready()),
        10: lambda: (c_stage(3),),
        12: lambda: (ready(3),),
    }
    first_solve = 8

    def tile_of(k, j):
        return a_ref[j % 2, j // 2, 4 * k : 4 * k + 4].reshape(WIDE, WIDE)

    def solve_tile(block, rows, j):
        here = pl.ds(j * WIDE, WIDE)
        done = pl.ds(0, j * WIDE)
        if j:
            block = block - dot3(
                dot_nt, (lh_ref[rows, done], ll_ref[rows, done]), (lh_ref[here, done], ll_ref[here, done])
            )
        low = split(dot3(dot_nt, split(block), (wh_ref[j], wl_ref[j])))
        lh_ref[rows, here] = low[0]
        ll_ref[rows, here] = low[1]

    column = lax.broadcasted_iota(jnp.int32, (WIDE, WIDE), 0)

    def solve_first(panel):
        at = pl.ds(pl.multiple_of(panel * WIDE, WIDE), WIDE)
        tile = jnp.concatenate([uv_ref[c % 2, c // 2, 1, :, at] for c in range(8)], axis=0).astype(f32)
        total_ref[:WIDE, :] = jnp.where(column < ri_ref[0], tile, 0.0)
        at = pl.ds(pl.multiple_of((panel % 4) * WIDE, WIDE), WIDE)
        tile = vj_all[:, :, :, at].astype(f32)
        tile = jnp.where(panel < 4, tile[:, :, :8], tile[:, :, 8:]).reshape(WIDE, WIDE)
        total_ref[WIDE:, :] = jnp.where(column < rj_ref[0], tile, 0.0)

    def solve_job(panel, n):
        side = n % 2
        tile = pl.ds(side * WIDE, WIDE)
        rows = pl.ds(ORDER + side * WIDE, WIDE)
        here = pl.ds(pl.multiple_of(panel * WIDE, WIDE), WIDE)
        if n < 14:
            at = pl.ds(n // 2 * WIDE, WIDE)
            total_ref[tile, :] = total_ref[tile, :] - dot3(
                dot_nt, (lh_ref[rows, at], ll_ref[rows, at]), (lh_ref[here, at], ll_ref[here, at])
            )
        else:
            low = split(dot3(dot_nt, split(total_ref[tile, :]), (wh_ref[panel], wl_ref[panel])))
            lh_ref[rows, here] = low[0]
            ll_ref[rows, here] = low[1]

    def half(h, carry):
        k = h // 2
        odd = h % 2

        for step, act in schedule.items():
            pl.when(h == step)(lambda act=act: (act(), None)[1])

        for static in range(STEPS):

            @pl.when((k == static) & (odd == 0))
            def _():
                here = pl.ds(static * WIDE, WIDE)
                done = pl.ds(0, static * WIDE)
                for j in range(static):
                    solve_tile(tile_of(static, j), here, j)
                block = tile_of(static, static)
                if static:
                    parts = (lh_ref[here, done], ll_ref[here, done])
                    block = block - dot3(dot_nt, parts, parts)
                d_ref[...] = block
                s_ref[...] = block[:HALF, :HALF]

        @pl.when(odd == 1)
        def _():
            low = dot3(dot_nt, split(d_ref[HALF:, :HALF]), split(w1_ref[...]))
            d_ref[HALF:, :HALF] = low
            parts = split(low)
            s_ref[...] = d_ref[HALF:, HALF:] - dot3(dot_nt, parts, parts)

        solving = (h >= first_solve) & (h < first_solve + STEPS - 1)

        @pl.when(solving)
        def _():
            solve_first(h - first_solve)
            invert_factor(s_ref, w2_ref, functools.partial(solve_job, h - first_solve))

        @pl.when(jnp.logical_not(solving))
        def _():
            invert_factor(s_ref, w2_ref)

        @pl.when(odd == 0)
        def _():
            w1_ref[...] = w2_ref[...]

        @pl.when(odd == 1)
        def _():
            first = split(w1_ref[...])
            second = split(w2_ref[...])
            corner = dot3(dot_nn, split(d_ref[HALF:, :HALF]), first)
            corner = split(-dot3(dot_nn, second, split(corner)))
            for part, w_ref in enumerate((wh_ref, wl_ref)):
                w_ref[k, :HALF, :HALF] = first[part]
                w_ref[k, :HALF, HALF:] = jnp.zeros((HALF, HALF), bf16)
                w_ref[k, HALF:, :HALF] = corner[part]
                w_ref[k, HALF:, HALF:] = second[part]

        return carry

    lax.fori_loop(0, 2 * STEPS, half, 0)

    rows_i = pl.ds(ORDER, WIDE)
    rows_j = pl.ds(ORDER + WIDE, WIDE)
    solve_first(STEPS - 1)
    for n in range(16):
        solve_job(STEPS - 1, n)

    product = dot_nt(lh_ref[rows_i, :], lh_ref[rows_j, :]).astype(bf16)
    width = solved_ref.shape[0]
    solved_ref[...] = lh_ref[pl.ds(pl.multiple_of(ORDER + col * width, width), width), :]
    for j in range(STEPS):
        at = pl.ds(j * WIDE, WIDE)
        left = jnp.concatenate([uv_ref[c % 2, c // 2, 0, :, at] for c in range(8)], axis=0)
        left = jnp.where(column < ri_ref[0], left, jnp.zeros_like(left))
        out_ref[at, :] = (-dot_tn(left, product)).astype(bf16)
    wait_sends()


def update_panel(rows_rank, cols_rank, diag_tile, left, right_i, right_j):
    scalar = pl.BlockSpec(memory_space=pltpu.SMEM)
    vmem = pl.BlockSpec(memory_space=pltpu.VMEM)
    dma = pltpu.SemaphoreType.DMA
    return pl.pallas_call(
        panel_kernel,
        out_shape=(jax.ShapeDtypeStruct((ORDER, WIDE), bf16), jax.ShapeDtypeStruct(right_i.shape, bf16)),
        in_specs=[scalar, scalar, vmem, vmem, vmem, vmem],
        out_specs=(vmem, vmem),
        scratch_shapes=[
            pltpu.VMEM((2, 4, 32, 64, WIDE), f32),
            pltpu.VMEM((2, 4, 2, 32, ORDER), bf16),
            pltpu.VMEM((4, 8, 16, ORDER // 2), bf16),
            pltpu.VMEM((ORDER + 2 * WIDE, ORDER), bf16),
            pltpu.VMEM((ORDER + 2 * WIDE, ORDER), bf16),
            pltpu.VMEM((STEPS, WIDE, WIDE), bf16),
            pltpu.VMEM((STEPS, WIDE, WIDE), bf16),
            pltpu.VMEM((WIDE, WIDE), f32),
            pltpu.VMEM((HALF, HALF), f32),
            pltpu.VMEM((HALF, HALF), f32),
            pltpu.VMEM((HALF, HALF), f32),
            pltpu.VMEM((2 * WIDE, WIDE), f32),
            dma((3,)), dma((4,)), dma((4, 3)), dma((4, 4)),
            dma((4, 7)), dma((4, 8)), dma((4, 3)), dma((4, 4)), dma((4,)), dma((4,)),
            dma((3,)), dma((4,)), dma((2,)), dma((7,)), dma((8,)), dma((3,)), dma((4,)),
        ],
        compiler_params=pltpu.CompilerParams(
            collective_id=0, has_side_effects=True, vmem_limit_bytes=58 * 2**20
        ),
    )(rows_rank, cols_rank, diag_tile, left, right_i, right_j)


def local(diag_tile, rows_left, rows_right, rows_rank, cols_right, cols_rank):
    update, solved = update_panel(
        rows_rank, cols_rank, diag_tile, rows_left[0].T, rows_right[0].T, cols_right[0].T
    )
    return update[None, None], solved.T[None]


def solution(mesh):
    placed = (
        P("row", "col"),
        P("row", None, "col"),
        P("row", None, "col"),
        P("row"),
        P("col", None, "row"),
        P("col"),
    )
    return jax.shard_map(
        local,
        mesh=mesh,
        in_specs=placed,
        out_specs=(P("row", "col", None, None), P("row", None, "col")),
        check_vma=False,
    )
```

```python
import functools

import jax
import jax.numpy as jnp
from jax import lax
from jax.experimental import pallas as pl
from jax.experimental.pallas import tpu as pltpu
from jax.sharding import PartitionSpec as P

f32 = jnp.float32
bf16 = jnp.bfloat16
ORDER = 2048
WIDE = 256
HALF = 128
STEPS = ORDER // WIDE
SLABS = 4
PIECE = 16
MESH = pl.DeviceIdType.MESH


def split(x):
    high = x.astype(bf16)
    return high, (x - high.astype(f32)).astype(bf16)


def dot_nt(a, b):
    return lax.dot_general(a, b, (((1,), (1,)), ((), ())), preferred_element_type=f32)


def dot_nn(a, b):
    return lax.dot_general(a, b, (((1,), (0,)), ((), ())), preferred_element_type=f32)


def dot_tn(a, b):
    return lax.dot_general(a, b, (((0,), (0,)), ((), ())), preferred_element_type=f32)


def dot3(dot, a, b):
    return dot(a[0], b[0]) + (dot(a[0], b[1]) + dot(a[1], b[0]))


def invert_factor(s_ref, w_ref, job=None):
    lane = lax.broadcasted_iota(jnp.int32, (8, HALF), 1)
    sub = lax.broadcasted_iota(jnp.int32, (8, HALF), 0)
    count = HALF // 8

    def spread(block, first):
        return [jnp.broadcast_to(block[:, first + c : first + c + 1], (8, HALF)) for c in range(8)]

    def one(value, r):
        return jnp.broadcast_to(value[r : r + 1, :], (8, HALF))

    diag = spread(s_ref[0:8, :], 0)
    under = spread(s_ref[8:16, :], 0)
    for group in range(count):
        first = 8 * group
        in_group = (lane >= first) & (lane < first + 8)
        rows = s_ref[first : first + 8, :]
        blocks = {q: s_ref[8 * q : 8 * q + 8, :] for q in range(group + 1, count)}
        if group + 1 < count:
            next_diag = spread(blocks[group + 1], first + 8)
        if group + 2 < count:
            next_under = spread(blocks[group + 2], first + 8)
        g = {}
        for c in range(8):
            for r in range(c + 1):
                g[r, c] = one(diag[c], r)
        inverse = []
        factor = {}
        for k in range(8):
            inverse.append(1.0 / g[k, k])
            for c in range(k + 1, 8):
                factor[k, c] = g[k, c] * inverse[k]
            for r in range(k + 1, 8):
                for c in range(r, 8):
                    g[r, c] = g[r, c] - factor[k, r] * g[k, c]

        def multipliers(columns):
            values, m = [], []
            for c in range(8):
                value = columns[c]
                for j in range(c):
                    value = value - m[j] * g[j, c]
                values.append(value)
                m.append(value * inverse[c])
            return values, m

        m_of = {}
        if group + 1 < count:
            values, m_of[group + 1] = multipliers(under)
            for c in range(8):
                for k in range(8):
                    pivot = one(values[k], c)
                    next_diag[c] = next_diag[c] - m_of[group + 1][k] * pivot
                    if group + 2 < count:
                        if k == 0 and c == 0:
                            m_of[group + 2] = multipliers(spread(blocks[group + 2], first))[1]
                        next_under[c] = next_under[c] - m_of[group + 2][k] * pivot
            diag = next_diag
            if group + 2 < count:
                under = next_under
        start = jnp.where(in_group, (lane - first == sub).astype(f32), rows)
        pivot_rows = []
        for k in range(8):
            row = one(start, k)
            for j in range(k):
                row = row - factor[j, k] * pivot_rows[j]
            pivot_rows.append(row)
        done = jnp.zeros((8, HALF), f32)
        for k in range(8):
            done = jnp.where(sub == k, pivot_rows[k] * lax.rsqrt(g[k, k]), done)
        w_ref[first : first + 8, :] = jnp.where(lane - first <= sub, done, 0.0)
        reduced = list(pivot_rows)
        if group + 3 < count:
            for k in reversed(range(8)):
                for j in range(k + 1, 8):
                    reduced[k] = reduced[k] - g[k, j] * reduced[j]
                reduced[k] = reduced[k] * inverse[k]
        for q, block in blocks.items():
            by = m_of[q] if q in m_of else spread(block, first)
            of = pivot_rows if q in m_of else reduced
            block = jnp.where(in_group, 0.0, block)
            for c in range(8):
                block = block - by[c] * of[c]
            s_ref[8 * q : 8 * q + 8, :] = block
        if job is not None:
            job(group)


def panel_kernel(
    ri_ref, rj_ref, diag_ref, left_ref, vi_ref, vj_ref, out_ref, solved_ref,
    a_ref, uv_ref, vj_all, lh_ref, ll_ref, wh_ref, wl_ref, d_ref, s_ref, w1_ref, w2_ref, total_ref, mixed_ref,
    first_send, first_recv, y_send, y_recv, z_send, z_recv, x_send, x_recv, c_send, c_recv,
    ux_send, ux_recv, uc_sem, jz_send, jz_recv, jy_send, jy_recv,
):
    row = lax.axis_index("row")
    col = lax.axis_index("col")
    y, z = row // 8, row % 8
    x, core = col // 2, col % 2
    sibling = (row, col + 1 - 2 * core)

    def along_x(d):
        return (x + d) % 4

    def along_y(d):
        return (y + d) % 4

    def along_z(d):
        return (z + d) % 8

    def at_x(to):
        return (row, 2 * to + core)

    def at_y(to):
        return (8 * to + z, col)

    def at_z(to):
        return (8 * y + to, col)

    def send(part, send_sem, recv_sem, device):
        return pltpu.make_async_remote_copy(
            src_ref=part, dst_ref=part, send_sem=send_sem, recv_sem=recv_sem, device_id=device, device_id_type=MESH
        )

    def deal_copy(d):
        to = jnp.where(core == 0, along_x(d), along_y(d))
        device = (jnp.where(core == 0, row, 8 * along_y(d) + z), jnp.where(core == 0, 2 * along_x(d), col))
        return pltpu.make_async_remote_copy(
            src_ref=diag_ref.at[pl.ds(PIECE * to, PIECE)],
            dst_ref=a_ref.at[core, x, row, pl.ds(PIECE * to, PIECE)],
            send_sem=first_send.at[d - 1],
            recv_sem=first_recv.at[jnp.where(core == 0, x, y)],
            device_id=device,
            device_id_type=MESH,
        )

    def mine(slab):
        return pl.ds(PIECE * jnp.where(core == 0, x, y), PIECE)

    def rows_part(slab, source, columns=None):
        columns = pl.ds(0, slab + 1) if columns is None else columns
        return a_ref.at[core, columns, 8 * slab + source, mine(slab)]

    def spread_copy(slab, d):
        return send(rows_part(slab, z), y_send.at[slab, d - 1], y_recv.at[slab, 0], at_y(along_y(d)))

    def spread_column(slab, d):
        return send(rows_part(slab, z, x), y_send.at[slab, d - 1], y_recv.at[slab, x], at_x(along_x(d)))

    def z_copy(slab, d):
        return send(rows_part(slab, z), z_send.at[slab, d - 1], z_recv.at[slab, z], at_z(along_z(d)))

    def last_part(slab, source):
        return a_ref.at[core, pl.ds(0, slab + 1), pl.ds(8 * slab, 8), pl.ds(PIECE * source, PIECE)]

    def last_copy(slab, d):
        at = jnp.where(core == 0, x, y)
        device = (jnp.where(core == 0, row, 8 * along_y(d) + z), jnp.where(core == 0, 2 * along_x(d), col))
        return send(last_part(slab, at), x_send.at[slab, d - 1], x_recv.at[slab, at], device)

    def c_copy(slab):
        part = a_ref.at[core, pl.ds(0, slab + 1), pl.ds(8 * slab, 8)]
        return send(part, c_send.at[slab], c_recv.at[slab], sibling)

    def first_stage():
        @pl.when(x <= y)
        def _():
            for d in range(1, 4):
                deal_copy(d).start()
            own = pl.ds(pl.multiple_of(PIECE * jnp.where(core == 0, x, y), PIECE), PIECE)
            a_ref[core, x, row, own] = diag_ref[own, :]

    def spread_stage():
        @pl.when(core == 0)
        def _():
            for source in range(4):
                @pl.when((source <= y) & (source != x))
                def _():
                    part = a_ref.at[core, source, row, mine(0)]
                    send(part, first_send.at[0], first_recv.at[source], sibling).wait_recv()

            for slab in range(SLABS):
                @pl.when(y == slab)
                def _():
                    for d in range(1, 4):
                        spread_copy(slab, d).start()

        @pl.when(core == 1)
        def _():
            for slab in range(SLABS):
                @pl.when((x <= slab) & (slab != y))
                def _():
                    send(rows_part(slab, z, x), first_send.at[0], first_recv.at[slab], sibling).wait_recv()

                @pl.when(x <= slab)
                def _():
                    for d in range(1, 4):
                        spread_column(slab, d).start()

    def z_stage(slab):
        @pl.when((core == 0) & (y != slab))
        def _():
            send(rows_part(slab, z), y_send.at[0, 0], y_recv.at[slab, 0], sibling).wait_recv()

        for source in range(slab + 1):
            @pl.when((core == 1) & (x != source))
            def _():
                send(rows_part(slab, z, source), y_send.at[0, 0], y_recv.at[slab, source], sibling).wait_recv()

        for d in range(1, 8):
            z_copy(slab, d).start()

    def last_stage(slab):
        for d in range(1, 8):
            source = along_z(d)
            send(rows_part(slab, source), z_send.at[slab, 0], z_recv.at[slab, source], sibling).wait_recv()
        for d in range(1, 4):
            last_copy(slab, d).start()

    def c_stage(slab):
        for d in range(1, 4):
            source = jnp.where(core == 0, along_x(d), along_y(d))
            send(last_part(slab, source), x_send.at[slab, 0], x_recv.at[slab, source], sibling).wait_recv()
        c_copy(slab).start()

    def ready(slab):
        part = a_ref.at[1 - core, pl.ds(0, slab + 1), pl.ds(8 * slab, 8)]
        send(part, c_send.at[slab], c_recv.at[slab], sibling).wait_recv()

    def ux_copy(d):
        return send(uv_ref.at[core, x], ux_send.at[d - 1], ux_recv.at[x], at_x(along_x(d)))

    def uc_copy():
        return send(uv_ref.at[core], uc_sem.at[0], uc_sem.at[1], sibling)

    def jz_copy(d):
        return send(vj_all.at[y, z], jz_send.at[d - 1], jz_recv.at[z], at_z(along_z(d)))

    def jy_copy(d):
        return send(vj_all.at[y], jy_send.at[d - 1], jy_recv.at[y], at_y(along_y(d)))

    def factors_first():
        for d in range(1, 8):
            jz_copy(d).start()
        for d in range(1, 4):
            ux_copy(d).start()

    def factors_second():
        for d in range(1, 8):
            source = along_z(d)
            send(vj_all.at[y, source], jz_send.at[0], jz_recv.at[source], sibling).wait_recv()
        for d in range(1, 4):
            jy_copy(d).start()
        for d in range(1, 4):
            source = along_x(d)
            send(uv_ref.at[core, source], ux_send.at[0], ux_recv.at[source], sibling).wait_recv()
        uc_copy().start()

    def factors_ready():
        for d in range(1, 4):
            source = along_y(d)
            send(vj_all.at[source], jy_send.at[0], jy_recv.at[source], sibling).wait_recv()
        send(uv_ref.at[1 - core], uc_sem.at[0], uc_sem.at[1], sibling).wait_recv()

    def wait_sends():
        @pl.when(x <= y)
        def _():
            for d in range(1, 4):
                deal_copy(d).wait_send()

        for slab in range(SLABS):
            @pl.when((core == 0) & (y == slab))
            def _():
                for d in range(1, 4):
                    spread_copy(slab, d).wait_send()

            @pl.when((core == 1) & (x <= slab))
            def _():
                for d in range(1, 4):
                    spread_column(slab, d).wait_send()

            for d in range(1, 8):
                z_copy(slab, d).wait_send()
            for d in range(1, 4):
                last_copy(slab, d).wait_send()
            c_copy(slab).wait_send()
        for d in range(1, 8):
            jz_copy(d).wait_send()
        for d in range(1, 4):
            jy_copy(d).wait_send()
            ux_copy(d).wait_send()
        uc_copy().wait_send()

    barrier = pltpu.get_barrier_semaphore()
    partners = [sibling]
    partners += [at_x(along_x(d)) for d in range(1, 4)]
    partners += [at_y(along_y(d)) for d in range(1, 4)]
    partners += [at_z(along_z(d)) for d in range(1, 8)]
    for device in partners:
        pl.semaphore_signal(barrier, inc=1, device_id=device, device_id_type=MESH)

    @pl.loop(0, lh_ref.shape[0] // WIDE)
    def _(tile):
        rows = pl.ds(pl.multiple_of(tile * WIDE, WIDE), WIDE)
        lh_ref[rows, :] = jnp.zeros((WIDE, ORDER), bf16)
        ll_ref[rows, :] = jnp.zeros((WIDE, ORDER), bf16)

    wh_ref[...] = jnp.zeros_like(wh_ref)
    wl_ref[...] = jnp.zeros_like(wl_ref)
    pl.semaphore_wait(barrier, len(partners))

    first_stage()
    uv_ref[core, x, 0] = left_ref[...]
    uv_ref[core, x, 1] = vi_ref[...]
    own = vj_ref[...].astype(f32)
    vj_all[y, z] = jnp.concatenate([own[:, : ORDER // 2], own[:, ORDER // 2 :]], axis=0).astype(bf16)
    spread_stage()
    z_stage(0)
    z_stage(1)
    last_stage(0)
    factors_first()
    c_stage(0)
    ready(0)

    schedule = {
        1: lambda: (last_stage(1), z_stage(2)),
        2: lambda: (factors_second(),),
        3: lambda: (c_stage(1), last_stage(2), z_stage(3)),
        4: lambda: (ready(1),),
        6: lambda: (last_stage(3),),
        7: lambda: (c_stage(2),),
        8: lambda: (ready(2), factors_ready()),
        9: lambda: (c_stage(3),),
        12: lambda: (ready(3),),
    }
    first_solve = 8

    def tile_of(k, j):
        return a_ref[j % 2, j // 2, 4 * k : 4 * k + 4].reshape(WIDE, WIDE)

    def spans(j):
        return [pl.ds(0, (j - 1) * WIDE)] * (j > 1) + [pl.ds((j - 1) * WIDE, WIDE)] * (j > 0)

    def solve_tile(block, rows, j):
        here = pl.ds(j * WIDE, WIDE)
        for done in spans(j):
            block = block - dot3(
                dot_nt, (lh_ref[rows, done], ll_ref[rows, done]), (lh_ref[here, done], ll_ref[here, done])
            )
        low = split(dot3(dot_nt, split(block), (wh_ref[j], wl_ref[j])))
        lh_ref[rows, here] = low[0]
        ll_ref[rows, here] = low[1]

    column = lax.broadcasted_iota(jnp.int32, (WIDE, WIDE), 0)

    def solve_first(panel):
        at = pl.ds(pl.multiple_of(panel * WIDE, WIDE), WIDE)
        tile = jnp.concatenate([uv_ref[c % 2, c // 2, 1, :, at] for c in range(8)], axis=0).astype(f32)
        total_ref[:WIDE, :] = jnp.where(column < ri_ref[0], tile, 0.0)
        at = pl.ds(pl.multiple_of((panel % 4) * WIDE, WIDE), WIDE)
        tile = vj_all[:, :, :, at].astype(f32)
        tile = jnp.where(panel < 4, tile[:, :, :8], tile[:, :, 8:]).reshape(WIDE, WIDE)
        total_ref[WIDE:, :] = jnp.where(column < rj_ref[0], tile, 0.0)

    def solve_job(panel, n):
        if n not in (0, 6, 14, 15):
            return
        side = int(n in (6, 15))
        tile = pl.ds(side * WIDE, WIDE)
        rows = pl.ds(ORDER + side * WIDE, WIDE)
        here = pl.ds(pl.multiple_of(panel * WIDE, WIDE), WIDE)
        if n < 14:
            at = pl.ds(0, (STEPS - 1) * WIDE)
            total_ref[tile, :] = total_ref[tile, :] - dot3(
                dot_nt, (lh_ref[rows, at], ll_ref[rows, at]), (lh_ref[here, at], ll_ref[here, at])
            )
        else:
            low = split(dot3(dot_nt, split(total_ref[tile, :]), (wh_ref[panel], wl_ref[panel])))
            lh_ref[rows, here] = low[0]
            ll_ref[rows, here] = low[1]

    def mix_job(n):
        if n == 1:
            mixed_ref[...] = dot3(dot_nn, split(d_ref[HALF:, :HALF]), split(w1_ref[...]))

    def half(h, carry):
        k = h // 2
        odd = h % 2

        for step, act in schedule.items():
            pl.when(h == step)(lambda act=act: (act(), None)[1])

        for static in range(STEPS):

            @pl.when((k == static) & (odd == 0))
            def _():
                here = pl.ds(static * WIDE, WIDE)
                if static % 2:
                    solve_tile(tile_of(static, static - 1), here, static - 1)
                else:
                    both = pl.ds(static * WIDE, 2 * WIDE)
                    for j in range(static):
                        pair = a_ref[j % 2, j // 2, 4 * static : 4 * static + 8].reshape(2 * WIDE, WIDE)
                        solve_tile(pair, both, j)
                block = tile_of(static, static)
                for done in spans(static):
                    parts = (lh_ref[here, done], ll_ref[here, done])
                    block = block - dot3(dot_nt, parts, parts)
                d_ref[...] = block
                s_ref[...] = block[:HALF, :HALF]

        @pl.when(odd == 1)
        def _():
            low = dot3(dot_nt, split(d_ref[HALF:, :HALF]), split(w1_ref[...]))
            d_ref[HALF:, :HALF] = low
            parts = split(low)
            s_ref[...] = d_ref[HALF:, HALF:] - dot3(dot_nt, parts, parts)

        solving = h >= first_solve

        @pl.when(solving)
        def _():
            solve_first(h - first_solve)

            def job(n):
                mix_job(n)
                solve_job(h - first_solve, n)

            invert_factor(s_ref, w2_ref, job)

        @pl.when(jnp.logical_not(solving))
        def _():
            invert_factor(s_ref, w2_ref, mix_job)

        @pl.when(odd == 0)
        def _():
            w1_ref[...] = w2_ref[...]

        @pl.when(odd == 1)
        def _():
            first = split(w1_ref[...])
            second = split(w2_ref[...])
            corner = split(-dot3(dot_nn, second, split(mixed_ref[...])))
            for part, w_ref in enumerate((wh_ref, wl_ref)):
                w_ref[k, :HALF, :HALF] = first[part]
                w_ref[k, :HALF, HALF:] = jnp.zeros((HALF, HALF), bf16)
                w_ref[k, HALF:, :HALF] = corner[part]
                w_ref[k, HALF:, HALF:] = second[part]

        return carry

    lax.fori_loop(0, 2 * STEPS, half, 0)

    rows_i = pl.ds(ORDER, WIDE)
    rows_j = pl.ds(ORDER + WIDE, WIDE)
    for n in (14, 15):
        solve_job(STEPS - 1, n)

    product = dot_nt(lh_ref[rows_i, :], lh_ref[rows_j, :]).astype(bf16)
    width = solved_ref.shape[0]
    solved_ref[...] = lh_ref[pl.ds(pl.multiple_of(ORDER + col * width, width), width), :]
    for j in range(STEPS):
        at = pl.ds(j * WIDE, WIDE)
        left = jnp.concatenate([uv_ref[c % 2, c // 2, 0, :, at] for c in range(8)], axis=0)
        left = jnp.where(column < ri_ref[0], left, jnp.zeros_like(left))
        out_ref[at, :] = (-dot_tn(left, product)).astype(bf16)
    wait_sends()


def update_panel(rows_rank, cols_rank, diag_tile, left, right_i, right_j):
    scalar = pl.BlockSpec(memory_space=pltpu.SMEM)
    vmem = pl.BlockSpec(memory_space=pltpu.VMEM)
    dma = pltpu.SemaphoreType.DMA
    return pl.pallas_call(
        panel_kernel,
        out_shape=(jax.ShapeDtypeStruct((ORDER, WIDE), bf16), jax.ShapeDtypeStruct(right_i.shape, bf16)),
        in_specs=[scalar, scalar, vmem, vmem, vmem, vmem],
        out_specs=(vmem, vmem),
        scratch_shapes=[
            pltpu.VMEM((2, 4, 32, 64, WIDE), f32),
            pltpu.VMEM((2, 4, 2, 32, ORDER), bf16),
            pltpu.VMEM((4, 8, 16, ORDER // 2), bf16),
            pltpu.VMEM((ORDER + 2 * WIDE, ORDER), bf16),
            pltpu.VMEM((ORDER + 2 * WIDE, ORDER), bf16),
            pltpu.VMEM((STEPS, WIDE, WIDE), bf16),
            pltpu.VMEM((STEPS, WIDE, WIDE), bf16),
            pltpu.VMEM((WIDE, WIDE), f32),
            pltpu.VMEM((HALF, HALF), f32),
            pltpu.VMEM((HALF, HALF), f32),
            pltpu.VMEM((HALF, HALF), f32),
            pltpu.VMEM((2 * WIDE, WIDE), f32),
            pltpu.VMEM((HALF, HALF), f32),
            dma((3,)), dma((4,)), dma((4, 3)), dma((4, 4)),
            dma((4, 7)), dma((4, 8)), dma((4, 3)), dma((4, 4)), dma((4,)), dma((4,)),
            dma((3,)), dma((4,)), dma((2,)), dma((7,)), dma((8,)), dma((3,)), dma((4,)),
        ],
        compiler_params=pltpu.CompilerParams(
            collective_id=0, has_side_effects=True, vmem_limit_bytes=58 * 2**20
        ),
    )(rows_rank, cols_rank, diag_tile, left, right_i, right_j)


def local(diag_tile, rows_left, rows_right, rows_rank, cols_right, cols_rank):
    update, solved = update_panel(
        rows_rank, cols_rank, diag_tile, rows_left[0].T, rows_right[0].T, cols_right[0].T
    )
    return update[None, None], solved.T[None]


def solution(mesh):
    placed = (
        P("row", "col"),
        P("row", None, "col"),
        P("row", None, "col"),
        P("row"),
        P("col", None, "row"),
        P("col"),
    )
    return jax.shard_map(
        local,
        mesh=mesh,
        in_specs=placed,
        out_specs=(P("row", "col", None, None), P("row", None, "col")),
        check_vma=False,
    )
```

```python
import functools

import jax
import jax.numpy as jnp
from jax import lax
from jax.experimental import pallas as pl
from jax.experimental.pallas import tpu as pltpu
from jax.sharding import PartitionSpec as P

f32 = jnp.float32
bf16 = jnp.bfloat16
ORDER = 2048
WIDE = 256
HALF = 128
STEPS = ORDER // WIDE
SLABS = 4
PIECE = 16
MESH = pl.DeviceIdType.MESH


def split(x):
    high = x.astype(bf16)
    return high, (x - high.astype(f32)).astype(bf16)


def dot_nt(a, b):
    return lax.dot_general(a, b, (((1,), (1,)), ((), ())), preferred_element_type=f32)


def dot_nn(a, b):
    return lax.dot_general(a, b, (((1,), (0,)), ((), ())), preferred_element_type=f32)


def dot_tn(a, b):
    return lax.dot_general(a, b, (((0,), (0,)), ((), ())), preferred_element_type=f32)


def dot3(dot, a, b):
    return dot(a[0], b[0]) + (dot(a[0], b[1]) + dot(a[1], b[0]))


def invert_factor(s_ref, w_ref, job=None):
    lane = lax.broadcasted_iota(jnp.int32, (8, HALF), 1)
    sub = lax.broadcasted_iota(jnp.int32, (8, HALF), 0)
    count = HALF // 8

    def spread(block, first):
        return [jnp.broadcast_to(block[:, first + c : first + c + 1], (8, HALF)) for c in range(8)]

    def one(value, r):
        return jnp.broadcast_to(value[r : r + 1, :], (8, HALF))

    diag = spread(s_ref[0:8, :], 0)
    under = spread(s_ref[8:16, :], 0)
    for group in range(count):
        first = 8 * group
        in_group = (lane >= first) & (lane < first + 8)
        rows = s_ref[first : first + 8, :]
        blocks = {q: s_ref[8 * q : 8 * q + 8, :] for q in range(group + 1, count)}
        if group + 1 < count:
            next_diag = spread(blocks[group + 1], first + 8)
        if group + 2 < count:
            next_under = spread(blocks[group + 2], first + 8)
        g = {}
        for c in range(8):
            for r in range(c + 1):
                g[r, c] = one(diag[c], r)
        inverse = []
        factor = {}
        for k in range(8):
            inverse.append(1.0 / g[k, k])
            for c in range(k + 1, 8):
                factor[k, c] = g[k, c] * inverse[k]
            for r in range(k + 1, 8):
                for c in range(r, 8):
                    g[r, c] = g[r, c] - factor[k, r] * g[k, c]

        def multipliers(columns):
            values, m = [], []
            for c in range(8):
                value = columns[c]
                for j in range(c):
                    value = value - m[j] * g[j, c]
                values.append(value)
                m.append(value * inverse[c])
            return values, m

        m_of = {}
        if group + 1 < count:
            values, m_of[group + 1] = multipliers(under)
            for c in range(8):
                for k in range(8):
                    pivot = one(values[k], c)
                    next_diag[c] = next_diag[c] - m_of[group + 1][k] * pivot
                    if group + 2 < count:
                        if k == 0 and c == 0:
                            m_of[group + 2] = multipliers(spread(blocks[group + 2], first))[1]
                        next_under[c] = next_under[c] - m_of[group + 2][k] * pivot
            diag = next_diag
            if group + 2 < count:
                under = next_under
        start = jnp.where(in_group, (lane - first == sub).astype(f32), rows)
        pivot_rows = []
        for k in range(8):
            row = one(start, k)
            for j in range(k):
                row = row - factor[j, k] * pivot_rows[j]
            pivot_rows.append(row)
        done = jnp.zeros((8, HALF), f32)
        for k in range(8):
            done = jnp.where(sub == k, pivot_rows[k] * lax.rsqrt(g[k, k]), done)
        w_ref[first : first + 8, :] = jnp.where(lane - first <= sub, done, 0.0)
        reduced = list(pivot_rows)
        if group + 3 < count:
            for k in reversed(range(8)):
                for j in range(k + 1, 8):
                    reduced[k] = reduced[k] - g[k, j] * reduced[j]
                reduced[k] = reduced[k] * inverse[k]
        for q, block in blocks.items():
            by = m_of[q] if q in m_of else spread(block, first)
            of = pivot_rows if q in m_of else reduced
            block = jnp.where(in_group, 0.0, block)
            for c in range(8):
                block = block - by[c] * of[c]
            s_ref[8 * q : 8 * q + 8, :] = block
        if job is not None:
            job(group)


def panel_kernel(
    ri_ref, rj_ref, diag_hbm, left_hbm, vi_hbm, vj_ref, out_ref, solved_ref,
    diag_ref, in_sem, a_ref, uv_ref, vj_all, lh_ref, ll_ref, wh_ref, wl_ref, d_ref, s_ref, w1_ref, w2_ref, total_ref, mixed_ref,
    first_send, first_recv, y_send, y_recv, z_send, z_recv, x_send, x_recv, c_send, c_recv,
    ux_send, ux_recv, uc_sem, jz_send, jz_recv, jy_send, jy_recv,
):
    row = lax.axis_index("row")
    col = lax.axis_index("col")
    y, z = row // 8, row % 8
    x, core = col // 2, col % 2
    sibling = (row, col + 1 - 2 * core)

    def along_x(d):
        return (x + d) % 4

    def along_y(d):
        return (y + d) % 4

    def along_z(d):
        return (z + d) % 8

    def at_x(to):
        return (row, 2 * to + core)

    def at_y(to):
        return (8 * to + z, col)

    def at_z(to):
        return (8 * y + to, col)

    def send(part, send_sem, recv_sem, device):
        return pltpu.make_async_remote_copy(
            src_ref=part, dst_ref=part, send_sem=send_sem, recv_sem=recv_sem, device_id=device, device_id_type=MESH
        )

    def deal_copy(d):
        to = jnp.where(core == 0, along_x(d), along_y(d))
        device = (jnp.where(core == 0, row, 8 * along_y(d) + z), jnp.where(core == 0, 2 * along_x(d), col))
        return pltpu.make_async_remote_copy(
            src_ref=diag_ref.at[pl.ds(PIECE * to, PIECE)],
            dst_ref=a_ref.at[core, x, row, pl.ds(PIECE * to, PIECE)],
            send_sem=first_send.at[d - 1],
            recv_sem=first_recv.at[jnp.where(core == 0, x, y)],
            device_id=device,
            device_id_type=MESH,
        )

    def mine(slab):
        return pl.ds(PIECE * jnp.where(core == 0, x, y), PIECE)

    def rows_part(slab, source, columns=None):
        columns = pl.ds(0, slab + 1) if columns is None else columns
        return a_ref.at[core, columns, 8 * slab + source, mine(slab)]

    def spread_copy(slab, d):
        return send(rows_part(slab, z), y_send.at[slab, d - 1], y_recv.at[slab, 0], at_y(along_y(d)))

    def spread_column(slab, d):
        return send(rows_part(slab, z, x), y_send.at[slab, d - 1], y_recv.at[slab, x], at_x(along_x(d)))

    def z_copy(slab, d):
        return send(rows_part(slab, z), z_send.at[slab, d - 1], z_recv.at[slab, z], at_z(along_z(d)))

    def last_part(slab, source):
        return a_ref.at[core, pl.ds(0, slab + 1), pl.ds(8 * slab, 8), pl.ds(PIECE * source, PIECE)]

    def last_copy(slab, d):
        at = jnp.where(core == 0, x, y)
        device = (jnp.where(core == 0, row, 8 * along_y(d) + z), jnp.where(core == 0, 2 * along_x(d), col))
        return send(last_part(slab, at), x_send.at[slab, d - 1], x_recv.at[slab, at], device)

    def c_copy(slab):
        part = a_ref.at[core, pl.ds(0, slab + 1), pl.ds(8 * slab, 8)]
        return send(part, c_send.at[slab], c_recv.at[slab], sibling)

    def first_stage():
        @pl.when(x <= y)
        def _():
            for d in range(1, 4):
                deal_copy(d).start()
            own = pl.ds(pl.multiple_of(PIECE * jnp.where(core == 0, x, y), PIECE), PIECE)
            a_ref[core, x, row, own] = diag_ref[own, :]

    def spread_stage():
        @pl.when(core == 0)
        def _():
            for source in range(4):
                @pl.when((source <= y) & (source != x))
                def _():
                    part = a_ref.at[core, source, row, mine(0)]
                    send(part, first_send.at[0], first_recv.at[source], sibling).wait_recv()

            for slab in range(SLABS):
                @pl.when(y == slab)
                def _():
                    for d in range(1, 4):
                        spread_copy(slab, d).start()

        @pl.when(core == 1)
        def _():
            for slab in range(SLABS):
                @pl.when((x <= slab) & (slab != y))
                def _():
                    send(rows_part(slab, z, x), first_send.at[0], first_recv.at[slab], sibling).wait_recv()

                @pl.when(x <= slab)
                def _():
                    for d in range(1, 4):
                        spread_column(slab, d).start()

    def z_stage(slab):
        @pl.when((core == 0) & (y != slab))
        def _():
            send(rows_part(slab, z), y_send.at[0, 0], y_recv.at[slab, 0], sibling).wait_recv()

        for source in range(slab + 1):
            @pl.when((core == 1) & (x != source))
            def _():
                send(rows_part(slab, z, source), y_send.at[0, 0], y_recv.at[slab, source], sibling).wait_recv()

        for d in range(1, 8):
            z_copy(slab, d).start()

    def last_stage(slab):
        for d in range(1, 8):
            source = along_z(d)
            send(rows_part(slab, source), z_send.at[slab, 0], z_recv.at[slab, source], sibling).wait_recv()
        for d in range(1, 4):
            last_copy(slab, d).start()

    def c_stage(slab):
        for d in range(1, 4):
            source = jnp.where(core == 0, along_x(d), along_y(d))
            send(last_part(slab, source), x_send.at[slab, 0], x_recv.at[slab, source], sibling).wait_recv()
        c_copy(slab).start()

    def ready(slab):
        part = a_ref.at[1 - core, pl.ds(0, slab + 1), pl.ds(8 * slab, 8)]
        send(part, c_send.at[slab], c_recv.at[slab], sibling).wait_recv()

    def ux_copy(d):
        return send(uv_ref.at[core, x], ux_send.at[d - 1], ux_recv.at[x], at_x(along_x(d)))

    def uc_copy():
        return send(uv_ref.at[core], uc_sem.at[0], uc_sem.at[1], sibling)

    def jz_copy(d):
        return send(vj_all.at[y, z], jz_send.at[d - 1], jz_recv.at[z], at_z(along_z(d)))

    def jy_copy(d):
        return send(vj_all.at[y], jy_send.at[d - 1], jy_recv.at[y], at_y(along_y(d)))

    def factors_first():
        for d in range(1, 8):
            jz_copy(d).start()
        for d in range(1, 4):
            ux_copy(d).start()

    def factors_second():
        for d in range(1, 8):
            source = along_z(d)
            send(vj_all.at[y, source], jz_send.at[0], jz_recv.at[source], sibling).wait_recv()
        for d in (1, 3):
            jy_copy(d).start()
        for d in range(1, 4):
            source = along_x(d)
            send(uv_ref.at[core, source], ux_send.at[0], ux_recv.at[source], sibling).wait_recv()
        uc_copy().start()

    def factors_ready():
        for d in range(1, 4):
            source = along_y(d)
            send(vj_all.at[source], jy_send.at[0], jy_recv.at[source], sibling).wait_recv()
        send(uv_ref.at[1 - core], uc_sem.at[0], uc_sem.at[1], sibling).wait_recv()

    def wait_sends():
        @pl.when(x <= y)
        def _():
            for d in range(1, 4):
                deal_copy(d).wait_send()

        for slab in range(SLABS):
            @pl.when((core == 0) & (y == slab))
            def _():
                for d in range(1, 4):
                    spread_copy(slab, d).wait_send()

            @pl.when((core == 1) & (x <= slab))
            def _():
                for d in range(1, 4):
                    spread_column(slab, d).wait_send()

            for d in range(1, 8):
                z_copy(slab, d).wait_send()
            for d in range(1, 4):
                last_copy(slab, d).wait_send()
            c_copy(slab).wait_send()
        for d in range(1, 8):
            jz_copy(d).wait_send()
        for d in range(1, 4):
            jy_copy(d).wait_send()
            ux_copy(d).wait_send()
        uc_copy().wait_send()

    barrier = pltpu.get_barrier_semaphore()
    partners = [sibling]
    partners += [at_x(along_x(d)) for d in range(1, 4)]
    partners += [at_y(along_y(d)) for d in range(1, 4)]
    partners += [at_z(along_z(d)) for d in range(1, 8)]
    for device in partners:
        pl.semaphore_signal(barrier, inc=1, device_id=device, device_id_type=MESH)
    loads = [
        pltpu.make_async_copy(source, target, in_sem.at[n])
        for n, (source, target) in enumerate(
            ((diag_hbm, diag_ref), (left_hbm, uv_ref.at[core, x, 0]), (vi_hbm, uv_ref.at[core, x, 1]))
        )
    ]
    for load in loads:
        load.start()
    own = vj_ref[...].astype(f32)
    vj_all[y, z] = jnp.concatenate([own[:, : ORDER // 2], own[:, ORDER // 2 :]], axis=0).astype(bf16)
    for load in loads:
        load.wait()
    pl.semaphore_wait(barrier, len(partners))

    first_stage()
    spread_stage()
    z_stage(0)
    z_stage(1)
    for part_ref in (lh_ref, ll_ref):
        for panel in range(STEPS - 1):
            rows, later = pl.ds(panel * WIDE, WIDE), pl.ds(panel * WIDE, ORDER - panel * WIDE)
            part_ref[rows, later] = jnp.zeros((WIDE, ORDER - panel * WIDE), bf16)
        part_ref[ORDER:, :] = jnp.zeros((2 * WIDE, ORDER), bf16)
    wh_ref[...] = jnp.zeros_like(wh_ref)
    wl_ref[...] = jnp.zeros_like(wl_ref)
    last_stage(0)
    factors_first()
    c_stage(0)
    ready(0)

    schedule = {
        1: lambda: (last_stage(1), z_stage(2)),
        2: lambda: (factors_second(),),
        3: lambda: (c_stage(1), last_stage(2), z_stage(3)),
        4: lambda: (ready(1),),
        5: lambda: (jy_copy(2).start(),),
        6: lambda: (c_stage(2), last_stage(3)),
        8: lambda: (ready(2), factors_ready()),
        10: lambda: (c_stage(3),),
        12: lambda: (ready(3),),
    }
    first_solve = 8

    def tile_of(k, j):
        return a_ref[j % 2, j // 2, 4 * k : 4 * k + 4].reshape(WIDE, WIDE)

    def spans(j):
        return [pl.ds(0, (j - 1) * WIDE)] * (j > 1) + [pl.ds((j - 1) * WIDE, WIDE)] * (j > 0)

    def solve_tile(block, rows, j):
        here = pl.ds(j * WIDE, WIDE)
        for done in spans(j):
            block = block - dot3(
                dot_nt, (lh_ref[rows, done], ll_ref[rows, done]), (lh_ref[here, done], ll_ref[here, done])
            )
        low = split(dot3(dot_nt, split(block), (wh_ref[j], wl_ref[j])))
        lh_ref[rows, here] = low[0]
        ll_ref[rows, here] = low[1]

    column = lax.broadcasted_iota(jnp.int32, (WIDE, WIDE), 0)

    def solve_first(panel):
        at = pl.ds(pl.multiple_of(panel * WIDE, WIDE), WIDE)
        tile = jnp.concatenate([uv_ref[c % 2, c // 2, 1, :, at] for c in range(8)], axis=0).astype(f32)
        total_ref[:WIDE, :] = jnp.where(column < ri_ref[0], tile, 0.0)
        at = pl.ds(pl.multiple_of((panel % 4) * WIDE, WIDE), WIDE)
        tile = vj_all[:, :, :, at].astype(f32)
        tile = jnp.where(panel < 4, tile[:, :, :8], tile[:, :, 8:]).reshape(WIDE, WIDE)
        total_ref[WIDE:, :] = jnp.where(column < rj_ref[0], tile, 0.0)

    def solve_job(panel, n):
        if n not in (0, 6, 14, 15):
            return
        side = int(n in (6, 15))
        tile = pl.ds(side * WIDE, WIDE)
        rows = pl.ds(ORDER + side * WIDE, WIDE)
        here = pl.ds(pl.multiple_of(panel * WIDE, WIDE), WIDE)
        if n < 14:
            at = pl.ds(0, (STEPS - 1) * WIDE)
            total_ref[tile, :] = total_ref[tile, :] - dot3(
                dot_nt, (lh_ref[rows, at], ll_ref[rows, at]), (lh_ref[here, at], ll_ref[here, at])
            )
        else:
            low = split(dot3(dot_nt, split(total_ref[tile, :]), (wh_ref[panel], wl_ref[panel])))
            lh_ref[rows, here] = low[0]
            ll_ref[rows, here] = low[1]

    def mix_job(n):
        if n == 1:
            mixed_ref[...] = dot3(dot_nn, split(d_ref[HALF:, :HALF]), split(w1_ref[...]))

    def half(h, carry):
        k = h // 2
        odd = h % 2

        for step, act in schedule.items():
            pl.when(h == step)(lambda act=act: (act(), None)[1])

        for static in range(STEPS):

            @pl.when((k == static) & (odd == 0))
            def _():
                here = pl.ds(static * WIDE, WIDE)
                if static % 2:
                    solve_tile(tile_of(static, static - 1), here, static - 1)
                else:
                    both = pl.ds(static * WIDE, 2 * WIDE)
                    for j in range(static):
                        pair = a_ref[j % 2, j // 2, 4 * static : 4 * static + 8].reshape(2 * WIDE, WIDE)
                        solve_tile(pair, both, j)
                block = tile_of(static, static)
                for done in spans(static):
                    parts = (lh_ref[here, done], ll_ref[here, done])
                    block = block - dot3(dot_nt, parts, parts)
                d_ref[...] = block
                s_ref[...] = block[:HALF, :HALF]

        @pl.when(odd == 1)
        def _():
            low = dot3(dot_nt, split(d_ref[HALF:, :HALF]), split(w1_ref[...]))
            d_ref[HALF:, :HALF] = low
            parts = split(low)
            s_ref[...] = d_ref[HALF:, HALF:] - dot3(dot_nt, parts, parts)

        solving = h >= first_solve

        @pl.when(solving)
        def _():
            solve_first(h - first_solve)

            def job(n):
                mix_job(n)
                solve_job(h - first_solve, n)

            invert_factor(s_ref, w2_ref, job)

        @pl.when(jnp.logical_not(solving))
        def _():
            invert_factor(s_ref, w2_ref, mix_job)

        @pl.when(odd == 0)
        def _():
            w1_ref[...] = w2_ref[...]

        @pl.when(odd == 1)
        def _():
            first = split(w1_ref[...])
            second = split(w2_ref[...])
            corner = split(-dot3(dot_nn, second, split(mixed_ref[...])))
            for part, w_ref in enumerate((wh_ref, wl_ref)):
                w_ref[k, :HALF, :HALF] = first[part]
                w_ref[k, :HALF, HALF:] = jnp.zeros((HALF, HALF), bf16)
                w_ref[k, HALF:, :HALF] = corner[part]
                w_ref[k, HALF:, HALF:] = second[part]

        return carry

    lax.fori_loop(0, 2 * STEPS, half, 0)

    rows_i = pl.ds(ORDER, WIDE)
    rows_j = pl.ds(ORDER + WIDE, WIDE)
    for n in (14, 15):
        solve_job(STEPS - 1, n)

    product = dot_nt(lh_ref[rows_i, :], lh_ref[rows_j, :]).astype(bf16)
    width = solved_ref.shape[0]
    solved_ref[...] = lh_ref[pl.ds(pl.multiple_of(ORDER + col * width, width), width), :]
    for j in range(STEPS):
        at = pl.ds(j * WIDE, WIDE)
        left = jnp.concatenate([uv_ref[c % 2, c // 2, 0, :, at] for c in range(8)], axis=0)
        left = jnp.where(column < ri_ref[0], left, jnp.zeros_like(left))
        out_ref[at, :] = (-dot_tn(left, product)).astype(bf16)
    wait_sends()


def update_panel(rows_rank, cols_rank, diag_tile, left, right_i, right_j):
    scalar = pl.BlockSpec(memory_space=pltpu.SMEM)
    vmem = pl.BlockSpec(memory_space=pltpu.VMEM)
    anywhere = pl.BlockSpec(memory_space=pl.ANY)
    dma = pltpu.SemaphoreType.DMA
    return pl.pallas_call(
        panel_kernel,
        out_shape=(jax.ShapeDtypeStruct((ORDER, WIDE), bf16), jax.ShapeDtypeStruct(right_i.shape, bf16)),
        in_specs=[scalar, scalar, anywhere, anywhere, anywhere, vmem],
        out_specs=(vmem, vmem),
        scratch_shapes=[
            pltpu.VMEM(diag_tile.shape, f32),
            dma((3,)),
            pltpu.VMEM((2, 4, 32, 64, WIDE), f32),
            pltpu.VMEM((2, 4, 2, 32, ORDER), bf16),
            pltpu.VMEM((4, 8, 16, ORDER // 2), bf16),
            pltpu.VMEM((ORDER + 2 * WIDE, ORDER), bf16),
            pltpu.VMEM((ORDER + 2 * WIDE, ORDER), bf16),
            pltpu.VMEM((STEPS, WIDE, WIDE), bf16),
            pltpu.VMEM((STEPS, WIDE, WIDE), bf16),
            pltpu.VMEM((WIDE, WIDE), f32),
            pltpu.VMEM((HALF, HALF), f32),
            pltpu.VMEM((HALF, HALF), f32),
            pltpu.VMEM((HALF, HALF), f32),
            pltpu.VMEM((2 * WIDE, WIDE), f32),
            pltpu.VMEM((HALF, HALF), f32),
            dma((3,)), dma((4,)), dma((4, 3)), dma((4, 4)),
            dma((4, 7)), dma((4, 8)), dma((4, 3)), dma((4, 4)), dma((4,)), dma((4,)),
            dma((3,)), dma((4,)), dma((2,)), dma((7,)), dma((8,)), dma((3,)), dma((4,)),
        ],
        compiler_params=pltpu.CompilerParams(
            collective_id=0, has_side_effects=True, vmem_limit_bytes=58 * 2**20
        ),
    )(rows_rank, cols_rank, diag_tile, left, right_i, right_j)


def local(diag_tile, rows_left, rows_right, rows_rank, cols_right, cols_rank):
    update, solved = update_panel(
        rows_rank, cols_rank, diag_tile, rows_left[0].T, rows_right[0].T, cols_right[0].T
    )
    return update[None, None], solved.T[None]


def solution(mesh):
    placed = (
        P("row", "col"),
        P("row", None, "col"),
        P("row", None, "col"),
        P("row"),
        P("col", None, "row"),
        P("col"),
    )
    return jax.shard_map(
        local,
        mesh=mesh,
        in_specs=placed,
        out_specs=(P("row", "col", None, None), P("row", None, "col")),
        check_vma=False,
    )
```

```python
import functools

import jax
import jax.numpy as jnp
from jax import lax
from jax.experimental import pallas as pl
from jax.experimental.pallas import tpu as pltpu
from jax.sharding import PartitionSpec as P

f32 = jnp.float32
bf16 = jnp.bfloat16
ORDER = 2048
WIDE = 256
HALF = 128
STEPS = ORDER // WIDE
SLABS = 4
PIECE = 16
MESH = pl.DeviceIdType.MESH


def split(x):
    high = x.astype(bf16)
    return high, (x - high.astype(f32)).astype(bf16)


def dot_nt(a, b):
    return lax.dot_general(a, b, (((1,), (1,)), ((), ())), preferred_element_type=f32)


def dot_nn(a, b):
    return lax.dot_general(a, b, (((1,), (0,)), ((), ())), preferred_element_type=f32)


def dot_tn(a, b):
    return lax.dot_general(a, b, (((0,), (0,)), ((), ())), preferred_element_type=f32)


def dot3(dot, a, b):
    return dot(a[0], b[0]) + (dot(a[0], b[1]) + dot(a[1], b[0]))


def invert_factor(s_ref, w_ref, job=None):
    lane = lax.broadcasted_iota(jnp.int32, (8, HALF), 1)
    sub = lax.broadcasted_iota(jnp.int32, (8, HALF), 0)
    count = HALF // 8

    def spread(block, first):
        return [jnp.broadcast_to(block[:, first + c : first + c + 1], (8, HALF)) for c in range(8)]

    def one(value, r):
        return jnp.broadcast_to(value[r : r + 1, :], (8, HALF))

    diag = spread(s_ref[0:8, :], 0)
    under = spread(s_ref[8:16, :], 0)
    for group in range(count):
        first = 8 * group
        in_group = (lane >= first) & (lane < first + 8)
        rows = s_ref[first : first + 8, :]
        blocks = {q: s_ref[8 * q : 8 * q + 8, :] for q in range(group + 1, count)}
        if group + 1 < count:
            next_diag = spread(blocks[group + 1], first + 8)
        if group + 2 < count:
            next_under = spread(blocks[group + 2], first + 8)
        g = {}
        for c in range(8):
            for r in range(c + 1):
                g[r, c] = one(diag[c], r)
        inverse = []
        factor = {}
        for k in range(8):
            inverse.append(1.0 / g[k, k])
            for c in range(k + 1, 8):
                factor[k, c] = g[k, c] * inverse[k]
            for r in range(k + 1, 8):
                for c in range(r, 8):
                    g[r, c] = g[r, c] - factor[k, r] * g[k, c]

        def multipliers(columns):
            values, m = [], []
            for c in range(8):
                value = columns[c]
                for j in range(c):
                    value = value - m[j] * g[j, c]
                values.append(value)
                m.append(value * inverse[c])
            return values, m

        m_of = {}
        if group + 1 < count:
            values, m_of[group + 1] = multipliers(under)
            for c in range(8):
                for k in range(8):
                    pivot = one(values[k], c)
                    next_diag[c] = next_diag[c] - m_of[group + 1][k] * pivot
                    if group + 2 < count:
                        if k == 0 and c == 0:
                            m_of[group + 2] = multipliers(spread(blocks[group + 2], first))[1]
                        next_under[c] = next_under[c] - m_of[group + 2][k] * pivot
            diag = next_diag
            if group + 2 < count:
                under = next_under
        start = jnp.where(in_group, (lane - first == sub).astype(f32), rows)
        pivot_rows = []
        for k in range(8):
            row = one(start, k)
            for j in range(k):
                row = row - factor[j, k] * pivot_rows[j]
            pivot_rows.append(row)
        done = jnp.zeros((8, HALF), f32)
        for k in range(8):
            done = jnp.where(sub == k, pivot_rows[k] * lax.rsqrt(g[k, k]), done)
        w_ref[first : first + 8, :] = jnp.where(lane - first <= sub, done, 0.0)
        reduced = list(pivot_rows)
        if group + 3 < count:
            for k in reversed(range(8)):
                for j in range(k + 1, 8):
                    reduced[k] = reduced[k] - g[k, j] * reduced[j]
                reduced[k] = reduced[k] * inverse[k]
        for q, block in blocks.items():
            by = m_of[q] if q in m_of else spread(block, first)
            of = pivot_rows if q in m_of else reduced
            block = jnp.where(in_group, 0.0, block)
            for c in range(8):
                block = block - by[c] * of[c]
            s_ref[8 * q : 8 * q + 8, :] = block
        if job is not None:
            job(group)


def panel_kernel(
    ri_ref, rj_ref, diag_hbm, left_hbm, vi_hbm, vj_ref, out_ref, solved_ref,
    diag_ref, in_sem, a_ref, uv_ref, vj_all, lh_ref, ll_ref, wh_ref, wl_ref, d_ref, s_ref, w1_ref, w2_ref, total_ref, mixed_ref,
    first_send, first_recv, y_send, y_recv, z_send, z_recv, x_send, x_recv, c_send, c_recv,
    ux_send, ux_recv, uc_sem, jz_send, jz_recv, jy_send, jy_recv,
):
    row = lax.axis_index("row")
    col = lax.axis_index("col")
    y, z = row // 8, row % 8
    x, core = col // 2, col % 2
    sibling = (row, col + 1 - 2 * core)

    def along_x(d):
        return (x + d) % 4

    def along_y(d):
        return (y + d) % 4

    def along_z(d):
        return (z + d) % 8

    def at_x(to):
        return (row, 2 * to + core)

    def at_y(to):
        return (8 * to + z, col)

    def at_z(to):
        return (8 * y + to, col)

    def send(part, send_sem, recv_sem, device):
        return pltpu.make_async_remote_copy(
            src_ref=part, dst_ref=part, send_sem=send_sem, recv_sem=recv_sem, device_id=device, device_id_type=MESH
        )

    def deal_copy(d):
        to = jnp.where(core == 0, along_x(d), along_y(d))
        device = (jnp.where(core == 0, row, 8 * along_y(d) + z), jnp.where(core == 0, 2 * along_x(d), col))
        return pltpu.make_async_remote_copy(
            src_ref=diag_ref.at[pl.ds(PIECE * to, PIECE)],
            dst_ref=a_ref.at[core, x, row, pl.ds(PIECE * to, PIECE)],
            send_sem=first_send.at[d - 1],
            recv_sem=first_recv.at[jnp.where(core == 0, x, y)],
            device_id=device,
            device_id_type=MESH,
        )

    def mine(slab):
        return pl.ds(PIECE * jnp.where(core == 0, x, y), PIECE)

    def rows_part(slab, source, columns=None):
        columns = pl.ds(0, slab + 1) if columns is None else columns
        return a_ref.at[core, columns, 8 * slab + source, mine(slab)]

    def spread_copy(slab, d):
        return send(rows_part(slab, z), y_send.at[slab, d - 1], y_recv.at[slab, 0], at_y(along_y(d)))

    def spread_column(slab, d):
        return send(rows_part(slab, z, x), y_send.at[slab, d - 1], y_recv.at[slab, x], at_x(along_x(d)))

    def z_copy(slab, d):
        return send(rows_part(slab, z), z_send.at[slab, d - 1], z_recv.at[slab, z], at_z(along_z(d)))

    def last_part(slab, source):
        return a_ref.at[core, pl.ds(0, slab + 1), pl.ds(8 * slab, 8), pl.ds(PIECE * source, PIECE)]

    def last_copy(slab, d):
        at = jnp.where(core == 0, x, y)
        device = (jnp.where(core == 0, row, 8 * along_y(d) + z), jnp.where(core == 0, 2 * along_x(d), col))
        return send(last_part(slab, at), x_send.at[slab, d - 1], x_recv.at[slab, at], device)

    def c_copy(slab):
        part = a_ref.at[core, pl.ds(0, slab + 1), pl.ds(8 * slab, 8)]
        return send(part, c_send.at[slab], c_recv.at[slab], sibling)

    def first_stage():
        @pl.when(x <= y)
        def _():
            for d in range(1, 4):
                deal_copy(d).start()
            own = pl.ds(pl.multiple_of(PIECE * jnp.where(core == 0, x, y), PIECE), PIECE)
            a_ref[core, x, row, own] = diag_ref[own, :]

    def spread_stage():
        @pl.when(core == 0)
        def _():
            for source in range(4):
                @pl.when((source <= y) & (source != x))
                def _():
                    part = a_ref.at[core, source, row, mine(0)]
                    send(part, first_send.at[0], first_recv.at[source], sibling).wait_recv()

            for slab in range(SLABS):
                @pl.when(y == slab)
                def _():
                    for d in range(1, 4):
                        spread_copy(slab, d).start()

        @pl.when(core == 1)
        def _():
            for slab in range(SLABS):
                @pl.when((x <= slab) & (slab != y))
                def _():
                    send(rows_part(slab, z, x), first_send.at[0], first_recv.at[slab], sibling).wait_recv()

                @pl.when(x <= slab)
                def _():
                    for d in range(1, 4):
                        spread_column(slab, d).start()

    def z_stage(slab):
        @pl.when((core == 0) & (y != slab))
        def _():
            send(rows_part(slab, z), y_send.at[0, 0], y_recv.at[slab, 0], sibling).wait_recv()

        for source in range(slab + 1):
            @pl.when((core == 1) & (x != source))
            def _():
                send(rows_part(slab, z, source), y_send.at[0, 0], y_recv.at[slab, source], sibling).wait_recv()

        for d in range(1, 8):
            z_copy(slab, d).start()

    def last_stage(slab):
        for d in range(1, 8):
            source = along_z(d)
            send(rows_part(slab, source), z_send.at[slab, 0], z_recv.at[slab, source], sibling).wait_recv()
        for d in range(1, 4):
            last_copy(slab, d).start()

    def c_stage(slab):
        for d in range(1, 4):
            source = jnp.where(core == 0, along_x(d), along_y(d))
            send(last_part(slab, source), x_send.at[slab, 0], x_recv.at[slab, source], sibling).wait_recv()
        c_copy(slab).start()

    def ready(slab):
        part = a_ref.at[1 - core, pl.ds(0, slab + 1), pl.ds(8 * slab, 8)]
        send(part, c_send.at[slab], c_recv.at[slab], sibling).wait_recv()

    def ux_copy(d):
        return send(uv_ref.at[core, x], ux_send.at[d - 1], ux_recv.at[x], at_x(along_x(d)))

    def uc_copy():
        return send(uv_ref.at[core], uc_sem.at[0], uc_sem.at[1], sibling)

    def jz_copy(d):
        return send(vj_all.at[y, z], jz_send.at[d - 1], jz_recv.at[z], at_z(along_z(d)))

    def jy_copy(d):
        return send(vj_all.at[y], jy_send.at[d - 1], jy_recv.at[y], at_y(along_y(d)))

    def factors_first():
        for d in range(1, 8):
            jz_copy(d).start()
        for d in range(1, 4):
            ux_copy(d).start()

    def factors_second():
        for d in range(1, 8):
            source = along_z(d)
            send(vj_all.at[y, source], jz_send.at[0], jz_recv.at[source], sibling).wait_recv()
        for d in (1, 3):
            jy_copy(d).start()
        for d in range(1, 4):
            source = along_x(d)
            send(uv_ref.at[core, source], ux_send.at[0], ux_recv.at[source], sibling).wait_recv()
        uc_copy().start()

    def factors_ready():
        for d in range(1, 4):
            source = along_y(d)
            send(vj_all.at[source], jy_send.at[0], jy_recv.at[source], sibling).wait_recv()
        send(uv_ref.at[1 - core], uc_sem.at[0], uc_sem.at[1], sibling).wait_recv()

    def wait_sends():
        @pl.when(x <= y)
        def _():
            for d in range(1, 4):
                deal_copy(d).wait_send()

        for slab in range(SLABS):
            @pl.when((core == 0) & (y == slab))
            def _():
                for d in range(1, 4):
                    spread_copy(slab, d).wait_send()

            @pl.when((core == 1) & (x <= slab))
            def _():
                for d in range(1, 4):
                    spread_column(slab, d).wait_send()

            for d in range(1, 8):
                z_copy(slab, d).wait_send()
            for d in range(1, 4):
                last_copy(slab, d).wait_send()
            c_copy(slab).wait_send()
        for d in range(1, 8):
            jz_copy(d).wait_send()
        for d in range(1, 4):
            jy_copy(d).wait_send()
            ux_copy(d).wait_send()
        uc_copy().wait_send()

    barrier = pltpu.get_barrier_semaphore()
    partners = [sibling]
    partners += [at_x(along_x(d)) for d in range(1, 4)]
    partners += [at_y(along_y(d)) for d in range(1, 4)]
    partners += [at_z(along_z(d)) for d in range(1, 8)]
    for device in partners:
        pl.semaphore_signal(barrier, inc=1, device_id=device, device_id_type=MESH)
    loads = [
        pltpu.make_async_copy(source, target, in_sem.at[n])
        for n, (source, target) in enumerate(
            ((diag_hbm, diag_ref), (left_hbm, uv_ref.at[core, x, 0]), (vi_hbm, uv_ref.at[core, x, 1]))
        )
    ]
    for load in loads:
        load.start()
    own = vj_ref[...].astype(f32)
    vj_all[y, z] = jnp.concatenate([own[:, : ORDER // 2], own[:, ORDER // 2 :]], axis=0).astype(bf16)
    for load in loads:
        load.wait()
    pl.semaphore_wait(barrier, len(partners))

    first_stage()
    spread_stage()
    z_stage(0)
    for part_ref in (lh_ref, ll_ref):
        for panel in range(STEPS - 1):
            rows, later = pl.ds(panel * WIDE, WIDE), pl.ds(panel * WIDE, ORDER - panel * WIDE)
            part_ref[rows, later] = jnp.zeros((WIDE, ORDER - panel * WIDE), bf16)
        part_ref[ORDER:, :] = jnp.zeros((2 * WIDE, ORDER), bf16)
    wh_ref[...] = jnp.zeros_like(wh_ref)
    wl_ref[...] = jnp.zeros_like(wl_ref)
    last_stage(0)
    z_stage(1)
    factors_first()
    c_stage(0)
    ready(0)

    schedule = {
        1: lambda: (last_stage(1), z_stage(2)),
        2: lambda: (factors_second(),),
        3: lambda: (c_stage(1), last_stage(2), z_stage(3)),
        4: lambda: (ready(1),),
        5: lambda: (jy_copy(2).start(),),
        6: lambda: (c_stage(2), last_stage(3)),
        8: lambda: (ready(2), factors_ready()),
        10: lambda: (c_stage(3),),
        12: lambda: (ready(3),),
    }
    first_solve = 8

    def tile_of(k, j):
        return a_ref[j % 2, j // 2, 4 * k : 4 * k + 4].reshape(WIDE, WIDE)

    def spans(j):
        return [pl.ds(0, (j - 1) * WIDE)] * (j > 1) + [pl.ds((j - 1) * WIDE, WIDE)] * (j > 0)

    def solve_tile(block, rows, j):
        here = pl.ds(j * WIDE, WIDE)
        for done in spans(j):
            block = block - dot3(
                dot_nt, (lh_ref[rows, done], ll_ref[rows, done]), (lh_ref[here, done], ll_ref[here, done])
            )
        low = split(dot3(dot_nt, split(block), (wh_ref[j], wl_ref[j])))
        lh_ref[rows, here] = low[0]
        ll_ref[rows, here] = low[1]

    column = lax.broadcasted_iota(jnp.int32, (WIDE, WIDE), 0)

    def solve_first(panel):
        at = pl.ds(pl.multiple_of(panel * WIDE, WIDE), WIDE)
        tile = jnp.concatenate([uv_ref[c % 2, c // 2, 1, :, at] for c in range(8)], axis=0).astype(f32)
        total_ref[:WIDE, :] = jnp.where(column < ri_ref[0], tile, 0.0)
        at = pl.ds(pl.multiple_of((panel % 4) * WIDE, WIDE), WIDE)
        tile = vj_all[:, :, :, at].astype(f32)
        tile = jnp.where(panel < 4, tile[:, :, :8], tile[:, :, 8:]).reshape(WIDE, WIDE)
        total_ref[WIDE:, :] = jnp.where(column < rj_ref[0], tile, 0.0)

    def solve_job(panel, n):
        if n not in (0, 6, 14, 15):
            return
        side = int(n in (6, 15))
        tile = pl.ds(side * WIDE, WIDE)
        rows = pl.ds(ORDER + side * WIDE, WIDE)
        here = pl.ds(pl.multiple_of(panel * WIDE, WIDE), WIDE)
        if n < 14:
            at = pl.ds(0, (STEPS - 1) * WIDE)
            total_ref[tile, :] = total_ref[tile, :] - dot3(
                dot_nt, (lh_ref[rows, at], ll_ref[rows, at]), (lh_ref[here, at], ll_ref[here, at])
            )
        else:
            low = split(dot3(dot_nt, split(total_ref[tile, :]), (wh_ref[panel], wl_ref[panel])))
            lh_ref[rows, here] = low[0]
            ll_ref[rows, here] = low[1]

    def mix_job(n):
        if n == 1:
            mixed_ref[...] = dot3(dot_nn, split(d_ref[HALF:, :HALF]), split(w1_ref[...]))

    def half(h, carry):
        k = h // 2
        odd = h % 2

        for step, act in schedule.items():
            pl.when(h == step)(lambda act=act: (act(), None)[1])

        for static in range(STEPS):

            @pl.when((k == static) & (odd == 0))
            def _():
                here = pl.ds(static * WIDE, WIDE)
                if static % 2:
                    solve_tile(tile_of(static, static - 1), here, static - 1)
                else:
                    both = pl.ds(static * WIDE, 2 * WIDE)
                    for j in range(static):
                        pair = a_ref[j % 2, j // 2, 4 * static : 4 * static + 8].reshape(2 * WIDE, WIDE)
                        solve_tile(pair, both, j)
                block = tile_of(static, static)
                for done in spans(static):
                    parts = (lh_ref[here, done], ll_ref[here, done])
                    block = block - dot3(dot_nt, parts, parts)
                d_ref[...] = block
                s_ref[...] = block[:HALF, :HALF]

        @pl.when(odd == 1)
        def _():
            low = dot3(dot_nt, split(d_ref[HALF:, :HALF]), split(w1_ref[...]))
            d_ref[HALF:, :HALF] = low
            parts = split(low)
            s_ref[...] = d_ref[HALF:, HALF:] - dot3(dot_nt, parts, parts)

        solving = h >= first_solve

        @pl.when(solving)
        def _():
            solve_first(h - first_solve)

            def job(n):
                mix_job(n)
                solve_job(h - first_solve, n)

            invert_factor(s_ref, w2_ref, job)

        @pl.when(jnp.logical_not(solving))
        def _():
            invert_factor(s_ref, w2_ref, mix_job)

        @pl.when(odd == 0)
        def _():
            w1_ref[...] = w2_ref[...]

        @pl.when(odd == 1)
        def _():
            first = split(w1_ref[...])
            second = split(w2_ref[...])
            corner = split(-dot3(dot_nn, second, split(mixed_ref[...])))
            for part, w_ref in enumerate((wh_ref, wl_ref)):
                w_ref[k, :HALF, :HALF] = first[part]
                w_ref[k, :HALF, HALF:] = jnp.zeros((HALF, HALF), bf16)
                w_ref[k, HALF:, :HALF] = corner[part]
                w_ref[k, HALF:, HALF:] = second[part]

        return carry

    lax.fori_loop(0, 2 * STEPS, half, 0)

    rows_i = pl.ds(ORDER, WIDE)
    rows_j = pl.ds(ORDER + WIDE, WIDE)
    for n in (14, 15):
        solve_job(STEPS - 1, n)

    product = dot_nt(lh_ref[rows_i, :], lh_ref[rows_j, :]).astype(bf16)
    width = solved_ref.shape[0]
    solved_ref[...] = lh_ref[pl.ds(pl.multiple_of(ORDER + col * width, width), width), :]
    for j in range(STEPS):
        at = pl.ds(j * WIDE, WIDE)
        left = jnp.concatenate([uv_ref[c % 2, c // 2, 0, :, at] for c in range(8)], axis=0)
        left = jnp.where(column < ri_ref[0], left, jnp.zeros_like(left))
        out_ref[at, :] = (-dot_tn(left, product)).astype(bf16)
    wait_sends()


def update_panel(rows_rank, cols_rank, diag_tile, left, right_i, right_j):
    scalar = pl.BlockSpec(memory_space=pltpu.SMEM)
    vmem = pl.BlockSpec(memory_space=pltpu.VMEM)
    anywhere = pl.BlockSpec(memory_space=pl.ANY)
    dma = pltpu.SemaphoreType.DMA
    return pl.pallas_call(
        panel_kernel,
        out_shape=(jax.ShapeDtypeStruct((ORDER, WIDE), bf16), jax.ShapeDtypeStruct(right_i.shape, bf16)),
        in_specs=[scalar, scalar, anywhere, anywhere, anywhere, vmem],
        out_specs=(vmem, vmem),
        scratch_shapes=[
            pltpu.VMEM(diag_tile.shape, f32),
            dma((3,)),
            pltpu.VMEM((2, 4, 32, 64, WIDE), f32),
            pltpu.VMEM((2, 4, 2, 32, ORDER), bf16),
            pltpu.VMEM((4, 8, 16, ORDER // 2), bf16),
            pltpu.VMEM((ORDER + 2 * WIDE, ORDER), bf16),
            pltpu.VMEM((ORDER + 2 * WIDE, ORDER), bf16),
            pltpu.VMEM((STEPS, WIDE, WIDE), bf16),
            pltpu.VMEM((STEPS, WIDE, WIDE), bf16),
            pltpu.VMEM((WIDE, WIDE), f32),
            pltpu.VMEM((HALF, HALF), f32),
            pltpu.VMEM((HALF, HALF), f32),
            pltpu.VMEM((HALF, HALF), f32),
            pltpu.VMEM((2 * WIDE, WIDE), f32),
            pltpu.VMEM((HALF, HALF), f32),
            dma((3,)), dma((4,)), dma((4, 3)), dma((4, 4)),
            dma((4, 7)), dma((4, 8)), dma((4, 3)), dma((4, 4)), dma((4,)), dma((4,)),
            dma((3,)), dma((4,)), dma((2,)), dma((7,)), dma((8,)), dma((3,)), dma((4,)),
        ],
        compiler_params=pltpu.CompilerParams(
            collective_id=0, has_side_effects=True, vmem_limit_bytes=58 * 2**20
        ),
    )(rows_rank, cols_rank, diag_tile, left, right_i, right_j)


def local(diag_tile, rows_left, rows_right, rows_rank, cols_right, cols_rank):
    update, solved = update_panel(
        rows_rank, cols_rank, diag_tile, rows_left[0].T, rows_right[0].T, cols_right[0].T
    )
    return update[None, None], solved.T[None]


def solution(mesh):
    placed = (
        P("row", "col"),
        P("row", None, "col"),
        P("row", None, "col"),
        P("row"),
        P("col", None, "row"),
        P("col"),
    )
    return jax.shard_map(
        local,
        mesh=mesh,
        in_specs=placed,
        out_specs=(P("row", "col", None, None), P("row", None, "col")),
        check_vma=False,
    )
```
